128 devices in a mesh: shard: 4 (over y_lo, core), rep: 32 (over x, y_hi, z).
Axes of the slice: x: 4, y: 4 (y_hi: 2, y_lo: 2; y = y_hi * 2 + y_lo), z: 4, core: 2. Of those that a mesh axis runs over, the one named last changes fastest.
Arguments:
- tokens: bfloat16 [32, 512, 768], P('rep', 'shard'), may hold values from -6 to 6
- lengths: int32 [32, 4], P('rep'), may hold values from 1 to 509, as said below
- routes: int32 [32, 512], P('rep', 'shard'), may hold values from 0 to 3, as said below
- attn_in: bfloat16 [2, 768, 2304], P(None, 'shard'), may hold values from -0.21875 to 0.21875
- attn_proj: bfloat16 [2, 768, 768], P(None, 'shard'), may hold values from -0.875 to 0.875
- norm_first: float32 [2, 768], replicated, may hold values from 0.5 to 1.5
- norm_second: float32 [2, 768], replicated, may hold values from 0.5 to 1.5
- rel_bias: float32 [2, 32, 12], replicated, may hold values from -4 to 4
- router: bfloat16 [2, 768, 4], replicated, may hold values from -0.15625 to 0.15625
- expert_in: bfloat16 [2, 4, 768, 3072], P(None, 'shard'), may hold values from -0.21875 to 0.21875
- expert_out: bfloat16 [2, 4, 3072, 768], P(None, 'shard'), may hold values from -0.4375 to 0.4375
- cotangent: bfloat16 [32, 512, 768], P('rep', 'shard'), may hold values from -6 to 6
Outputs:
- result: bfloat16 [32, 512, 768], P('rep', 'shard')
- tokens_grad: bfloat16 [32, 512, 768], P('rep', 'shard')
- attn_in_grad: float32 [2, 768, 2304], P(None, ('shard', 'rep'))
- attn_proj_grad: float32 [2, 768, 768], P(None, ('shard', 'rep'))
- norm_first_grad: float32 [2, 768], P(None, ('shard', 'rep'))
- norm_second_grad: float32 [2, 768], P(None, ('shard', 'rep'))
- rel_bias_grad: float32 [2, 384], P(None, ('shard', 'rep'))
- router_grad: float32 [2, 768, 4], P(None, ('shard', 'rep'))
- expert_in_grad: float32 [2, 4, 768, 3072], P(None, 'shard', 'rep')
- expert_out_grad: float32 [2, 4, 3072, 768], P(None, 'shard', 'rep')
The draws below stay inside these ranges and needn't reach their ends.
Inputs may be any that keep to these rules, and one draw needn't show every extreme that they name: Each group's 4 lengths are positive and sum to 512; one of them exceeds 512 - 128. `routes`: among the 128 tokens of one device at most 64 name one expert; in each group one expert is named by exactly 64 tokens of every device of the group.
All inputs are finite; a program needn't handle non-finite values.
Results may differ from the reference program's by a relative error of at most 0.033.
Values may be sent and summed in bfloat16 or wider, within the bound.
No kernel may reach another device: no remote copies, remote signals or barrier semaphores. Data moves between devices by JAX's collectives and lax.ppermute only.
A program may use at most 256 MiB of HBM per device.

```python
import jax
import jax.numpy as jnp
from jax import lax

D = 768
H = 12
FF = 3072
NB = 32
LAYERS = 2
SEQS = 4
TOK_DEV = 128
GROUP_TOK = 512
GROUPS = 32
EXPERTS = 4
CAP = 64


def draw_lengths(key, part):
    key = jax.random.fold_in(key, 7)
    first_key, second_key, third_key = jax.random.split(key, 3)
    shorter = jax.random.randint(first_key, (GROUPS, SEQS), 1, TOK_DEV // 4 + 1)
    chosen_group = jax.random.randint(third_key, (), 0, GROUPS)
    shorter = jnp.where(jnp.arange(GROUPS)[:, None] == chosen_group, 1, shorter)
    longest = jax.random.randint(second_key, (GROUPS, 1), 0, SEQS)
    is_long = jnp.arange(SEQS)[None, :] == longest
    others = jnp.sum(jnp.where(is_long, 0, shorter), axis=1, keepdims=True)
    return jnp.where(is_long, GROUP_TOK - others, shorter).astype(jnp.int32)


def draw_routes(key, part):
    key = jax.random.fold_in(key, 11)
    heavy_key, order_key, other_key = jax.random.split(key, 3)
    blocks = GROUP_TOK // TOK_DEV
    heavy = jax.random.randint(heavy_key, (GROUPS, 1, 1), 0, EXPERTS)
    order_keys = jax.random.split(order_key, GROUPS * blocks)
    orders = jax.vmap(lambda subkey: jax.random.permutation(subkey, TOK_DEV))(order_keys).reshape(GROUPS, blocks, TOK_DEV)
    spread = jax.random.randint(other_key, (GROUPS, blocks, TOK_DEV), 1, EXPERTS)
    picked = jnp.where(orders < CAP, heavy, (heavy + spread) % EXPERTS)
    return picked.reshape(GROUPS, GROUP_TOK).astype(jnp.int32)


def block_scale(stream_key, extent, shards, smallest, largest):
    def one(dim, blocks):
        steps = jax.random.uniform(jax.random.fold_in(jax.random.fold_in(stream_key, 6), dim), (blocks,), jnp.float32, smallest / len(shards), largest / len(shards))
        return jnp.repeat(jnp.exp(steps), extent[dim] // blocks).reshape((-1,) + (1,) * (len(extent) - dim - 1))

    loudness = one(*shards[0])
    for cut in shards[1:]:
        loudness = loudness * one(*cut)
    return loudness


def noise(key, extent, scale, limit, pieces=(), kind=jnp.bfloat16):
    entries = scale * jax.random.normal(key, extent, jnp.float32)
    if pieces:
        entries = entries * block_scale(key, extent, pieces, -0.22, 0.18)
    return jnp.clip(entries, -limit, limit).astype(kind)


def setup_inputs(seed: int = 0) -> dict:
    arg_keys = jax.random.split(jax.random.key(seed), 13)
    tokens = noise(arg_keys[0], (GROUPS, GROUP_TOK, D), 1.0, 6.0, ((0, 32), (1, 4)))
    lengths = draw_lengths(jax.random.fold_in(arg_keys[12], 71), 0)
    routes = draw_routes(jax.random.fold_in(arg_keys[12], 71), 0)
    attn_in = noise(arg_keys[3], (LAYERS, D, 3 * D), D ** -0.5, 0.21875, ((1, 4),))
    attn_proj = noise(arg_keys[4], (LAYERS, D, D), (D // 16) ** -0.5, 0.875, ((1, 4),))
    norm_first = jnp.clip(1.0 + 0.1 * jax.random.normal(arg_keys[5], (LAYERS, D), jnp.float32), 0.5, 1.5)
    norm_second = jnp.clip(1.0 + 0.1 * jax.random.normal(arg_keys[6], (LAYERS, D), jnp.float32), 0.5, 1.5)
    rel_bias = noise(arg_keys[7], (LAYERS, NB, H), 1.0, 4.0, (), jnp.float32)
    router = noise(arg_keys[8], (LAYERS, D, EXPERTS), (2 * D) ** -0.5, 0.15625)
    expert_in = noise(arg_keys[9], (LAYERS, EXPERTS, D, FF), D ** -0.5, 0.21875, ((1, 4),))
    expert_out = noise(arg_keys[10], (LAYERS, EXPERTS, FF, D), (FF // 16) ** -0.5, 0.4375, ((1, 4),))
    cotangent = noise(arg_keys[11], (GROUPS, GROUP_TOK, D), 1.0, 6.0, ((0, 32), (1, 4)))
    return {"tokens": tokens, "lengths": lengths, "routes": routes, "attn_in": attn_in, "attn_proj": attn_proj, "norm_first": norm_first, "norm_second": norm_second, "rel_bias": rel_bias, "router": router, "expert_in": expert_in, "expert_out": expert_out, "cotangent": cotangent}


EPS = 1e-06
SCALE = 0.125
NEG = -1e+30
THRESHOLDS = (12, 16, 23, 32, 46, 64, 91)
HIGH = lax.Precision.HIGHEST

@jax.custom_vjp
def low(v):
    return lax.optimization_barrier(v.astype(jnp.bfloat16)).astype(jnp.float32)

@jax.custom_vjp
def low_back(v):
    return v

def low_keep(v):
    return (low(v), None)

def low_pass(kept, grad):
    return (grad,)

def back_keep(v):
    return (v, None)

def back_low(kept, grad):
    return (low(grad),)
low.defvjp(low_keep, low_pass)
low_back.defvjp(back_keep, back_low)

def bucket_of(offset):
    distance = jnp.abs(offset)
    far_bucket = 8 + sum(((distance >= threshold).astype(jnp.int32) for threshold in THRESHOLDS))
    bucket_id = jnp.where(distance < 8, distance, far_bucket)
    return bucket_id + 16 * (offset > 0).astype(jnp.int32)

def rms_norm(vector, gain_vec):
    return vector * lax.rsqrt(lax.optimization_barrier(jnp.mean(vector * vector, -1, keepdims=True)) + EPS) * gain_vec

def dispatch_table(route_rows, experts, capacity):
    onehot = (route_rows[..., None] == jnp.arange(experts, dtype=jnp.int32)).astype(jnp.int32)
    position = lax.optimization_barrier(jnp.sum(jnp.cumsum(onehot, axis=-2) * onehot, -1)) - 1
    target = route_rows * capacity + position
    return (jnp.arange(experts * capacity, dtype=jnp.int32)[:, None] == target[..., None, :]).astype(jnp.float32)

def group_forward(x_group, doc_group, route_group, bucket_ids, weights):
    w_qkv, w_proj, gain_first, gain_second, bias_rows, router_w, w_inner, w_outer = weights
    row_count, model_width = x_group.shape
    head_count = bias_rows.shape[2]
    head_size = model_width // head_count
    experts = router_w.shape[2]
    blocks, per_device = route_group.shape
    capacity = per_device // 2
    same_doc = doc_group[:, None] == doc_group[None, :]
    dispatch = dispatch_table(route_group, experts, capacity)
    chosen = (route_group.reshape(-1)[:, None] == jnp.arange(experts, dtype=jnp.int32)).astype(jnp.float32)
    stream = x_group
    for level in range(w_qkv.shape[0]):
        normed = low(rms_norm(stream, gain_first[level]))
        proj_qkv = low(low_back(jnp.dot(normed, w_qkv[level], precision=HIGH)))
        query_part = proj_qkv[:, :model_width].reshape(row_count, head_count, head_size)
        key_part = proj_qkv[:, model_width:2 * model_width].reshape(row_count, head_count, head_size)
        value_part = proj_qkv[:, 2 * model_width:].reshape(row_count, head_count, head_size)
        rel_terms = jnp.transpose(bias_rows[level][bucket_ids], (2, 0, 1))
        scores = jnp.einsum('ihd,jhd->hij', query_part, key_part, precision=HIGH) * SCALE + rel_terms
        scores = jnp.where(same_doc[None], low_back(scores), NEG)
        attn_probs = low(jax.nn.softmax(scores, axis=-1))
        attn_mixed = jnp.einsum('hij,jhd->ihd', attn_probs, value_part, precision=HIGH).reshape(row_count, model_width)
        attn_mixed = low(low_back(attn_mixed))
        stream = stream + low_back(jnp.dot(attn_mixed, w_proj[level], precision=HIGH))
        normed_two = low(rms_norm(stream, gain_second[level]))
        logits = jnp.dot(normed_two, router_w[level], precision=HIGH)
        gate_value = lax.optimization_barrier(jnp.sum(jax.nn.softmax(logits, -1) * chosen, -1))
        slot_rows = jnp.einsum('sct,std->scd', dispatch, normed_two.reshape(blocks, per_device, model_width), precision=HIGH)
        expert_rows = jnp.transpose(slot_rows.reshape(blocks, experts, capacity, model_width), (1, 0, 2, 3))
        expert_rows = low_back(expert_rows.reshape(experts, blocks * capacity, model_width))
        hidden = low_back(jnp.einsum('erd,edf->erf', expert_rows, w_inner[level], precision=HIGH))
        active = low(jax.nn.gelu(hidden, approximate=True))
        produced = low(low_back(jnp.einsum('erf,efd->erd', active, w_outer[level], precision=HIGH)))
        produced = jnp.transpose(produced.reshape(experts, blocks, capacity, model_width), (1, 0, 2, 3))
        produced = produced.reshape(blocks, experts * capacity, model_width)
        returned = jnp.einsum('sct,scd->std', dispatch, produced, precision=HIGH).reshape(row_count, model_width)
        stream = stream + gate_value[:, None] * returned
    return stream

def reference(tokens, lengths, routes, attn_in, attn_proj, norm_first, norm_second, rel_bias, router, expert_in, expert_out, cotangent):
    groups, group_tok, model_width = tokens.shape
    blocks = group_tok // TOK_DEV
    weights = tuple((array.astype(jnp.float32) for array in (attn_in, attn_proj, norm_first, norm_second, rel_bias, router, expert_in, expert_out)))
    positions = jnp.arange(group_tok, dtype=jnp.int32)
    bucket_ids = bucket_of(positions[None, :] - positions[:, None])
    ends = jnp.cumsum(lengths, axis=1).astype(jnp.int32)
    doc_ids = lax.optimization_barrier(jnp.sum((positions[None, :, None] >= ends[:, None, :]).astype(jnp.int32), -1))
    route_blocks = routes.reshape(groups, blocks, TOK_DEV)

    def forward(stream_in, params):

        def step_fn(carry, inputs):
            x_group, doc_group, route_group = inputs
            return (carry, jax.checkpoint(group_forward)(x_group, doc_group, route_group, bucket_ids, params))
        _, outputs = lax.scan(step_fn, jnp.zeros((), jnp.float32), (stream_in, doc_ids, route_blocks))
        return outputs
    result, pull_back = jax.vjp(forward, tokens.astype(jnp.float32), weights)
    tokens_grad, grads = pull_back(cotangent.astype(jnp.float32))
    grad_qkv, grad_proj, grad_first, grad_second, grad_bias, grad_router, grad_inner, grad_outer = grads
    return (result.astype(jnp.bfloat16), tokens_grad.astype(jnp.bfloat16), grad_qkv, grad_proj, grad_first, grad_second, grad_bias.reshape(grad_bias.shape[0], -1), grad_router, grad_inner, grad_outer)
```

```python
import functools

import jax
import jax.numpy as jnp
from jax import lax
from jax.experimental import pallas as pl
from jax.experimental.pallas import tpu as pltpu
from jax.sharding import PartitionSpec as P

EPS = 1e-06
SCALE = 0.125
NEG = -1e30
THRESHOLDS = (12, 16, 23, 32, 46, 64, 91)
HIGH = lax.Precision.HIGHEST
F32 = jnp.float32
BF16 = jnp.bfloat16
BLK = 128
NX, NY, NZ = 4, 2, 4


def bucket_of(offset):
    distance = jnp.abs(offset)
    far_bucket = 8 + sum(((distance >= threshold).astype(jnp.int32) for threshold in THRESHOLDS))
    bucket_id = jnp.where(distance < 8, distance, far_bucket)
    return bucket_id + 16 * (offset > 0).astype(jnp.int32)


def rms_norm(vector, gain_vec):
    inverse = lax.rsqrt(jnp.mean(vector * vector, -1, keepdims=True) + EPS)
    return vector * inverse * gain_vec


def norm_back(vector, gain_vec, upstream):
    inverse = lax.rsqrt(jnp.mean(vector * vector, -1, keepdims=True) + EPS)
    scaled = upstream * gain_vec
    grad_gain = jnp.sum(upstream * vector * inverse, 0)
    grad_in = inverse * scaled - vector * (inverse * inverse * inverse) * jnp.mean(
        scaled * vector, -1, keepdims=True
    )
    return (grad_in, grad_gain)


def gelu_tanh(vector):
    return jax.nn.gelu(vector, approximate=True)


def dot(a, b, dims=((1,), (0,))):
    return lax.dot_general(a, b, (dims, ((), ())), preferred_element_type=F32)


def attn_fwd_kernel(q_ref, k_ref, v_ref, bias_ref, docq_ref, dock_ref, o_ref, p_ref):
    tok = q_ref.shape[0]
    nblk = tok // BLK
    first = lax.broadcasted_iota(jnp.int32, (1, BLK), 1) < BLK // 2
    k = k_ref[...]
    v = v_ref[...]
    for i in range(nblk):
        rows = slice(i * BLK, (i + 1) * BLK)
        same = docq_ref[rows, :] == dock_ref[...]
        q = q_ref[rows, :]
        outs = []
        for hh in range(2):
            mine = first if hh == 0 else jnp.logical_not(first)
            qm = jnp.where(mine, q, jnp.zeros_like(q))
            s = dot(qm, k, ((1,), (1,))) * SCALE
            bias = jnp.concatenate(
                [bias_ref[hh, max(-2, min(2, j - i)) + 2] for j in range(nblk)], axis=1
            )
            s = jnp.where(same, s + bias, NEG)
            e = jnp.exp(s - jnp.max(s, -1, keepdims=True))
            p = (e * (1.0 / jnp.sum(e, -1, keepdims=True))).astype(BF16)
            p_ref[hh, rows, :] = p
            outs.append(dot(p, v))
        o_ref[rows, :] = jnp.where(first, outs[0], outs[1]).astype(BF16)


def attn_fwd(qkv, bias, docq, dock):
    tok, width = qkv.shape
    heads_w = width // 3
    pairs = heads_w // BLK
    return pl.pallas_call(
        attn_fwd_kernel,
        grid=(pairs,),
        in_specs=[
            pl.BlockSpec((tok, BLK), lambda h: (0, h)),
            pl.BlockSpec((tok, BLK), lambda h: (0, pairs + h)),
            pl.BlockSpec((tok, BLK), lambda h: (0, 2 * pairs + h)),
            pl.BlockSpec((2, 5, BLK, BLK), lambda h: (h, 0, 0, 0)),
            pl.BlockSpec((tok, 1), lambda h: (0, 0)),
            pl.BlockSpec((1, tok), lambda h: (0, 0)),
        ],
        out_specs=[
            pl.BlockSpec((tok, BLK), lambda h: (0, h)),
            pl.BlockSpec((2, tok, tok), lambda h: (h, 0, 0)),
        ],
        out_shape=[
            jax.ShapeDtypeStruct((tok, heads_w), BF16),
            jax.ShapeDtypeStruct((2 * pairs, tok, tok), BF16),
        ],
        compiler_params=pltpu.CompilerParams(vmem_limit_bytes=40 * 1024 * 1024),
        cost_estimate=pl.CostEstimate(
            flops=8 * tok * tok * heads_w,
            bytes_accessed=8 * tok * width + 4 * pairs * tok * tok,
            transcendentals=2 * pairs * tok * tok,
        ),
        name="attn_fwd",
    )(qkv, qkv, qkv, bias, docq, dock)


def attn_bwd_kernel(q_ref, k_ref, v_ref, p_ref, do_ref, o_ref, dqkv_ref, m_ref, ds_ref):
    tok = q_ref.shape[0]
    nblk = tok // BLK
    pairs = pl.num_programs(0)
    step = pl.program_id(0)
    first = lax.broadcasted_iota(jnp.int32, (1, BLK), 1) < BLK // 2
    k = k_ref[...]
    v = v_ref[...]
    q = q_ref[...]
    do = do_ref[...]
    dk = jnp.zeros((tok, BLK), F32)
    dv = jnp.zeros((tok, BLK), F32)
    dqs = []
    for hh in range(2):
        mine = first if hh == 0 else jnp.logical_not(first)
        dom = jnp.where(mine, do, jnp.zeros_like(do))
        qm = jnp.where(mine, q, jnp.zeros_like(q))
        parts = [None] * 5
        dq_rows = []
        for i in range(nblk):
            rows = slice(i * BLK, (i + 1) * BLK)
            doi = dom[rows, :]
            dp = dot(doi, v, ((1,), (1,)))
            base = jnp.sum(
                doi.astype(F32) * o_ref[rows, :].astype(F32), -1, keepdims=True
            )
            ds = p_ref[hh, rows, :].astype(F32) * (dp - base)
            for j in range(nblk):
                d = max(-2, min(2, j - i)) + 2
                piece = ds[:, j * BLK : (j + 1) * BLK]
                parts[d] = piece if parts[d] is None else parts[d] + piece
            dsb = ds.astype(BF16)
            ds_ref[rows, :] = dsb
            dq_rows.append(dot(dsb, k))
        for d in range(5):
            m_ref[hh, d] = parts[d].astype(BF16)
        dqs.append(dq_rows)
        dk = dk + dot(ds_ref[...], qm, ((0,), (0,)))
        dv = dv + dot(p_ref[hh], dom, ((0,), (0,)))
    at = lambda part: pl.ds(pl.multiple_of((part * pairs + step) * BLK, BLK), BLK)
    for i in range(nblk):
        rows = slice(i * BLK, (i + 1) * BLK)
        dqkv_ref[rows, at(0)] = (jnp.where(first, dqs[0][i], dqs[1][i]) * SCALE).astype(BF16)
    dqkv_ref[:, at(1)] = (dk * SCALE).astype(BF16)
    dqkv_ref[:, at(2)] = dv.astype(BF16)


def attn_bwd(qkv, p, do, o):
    tok, width = qkv.shape
    heads_w = width // 3
    pairs = heads_w // BLK
    return pl.pallas_call(
        attn_bwd_kernel,
        grid=(pairs,),
        in_specs=[
            pl.BlockSpec((tok, BLK), lambda h: (0, h)),
            pl.BlockSpec((tok, BLK), lambda h: (0, pairs + h)),
            pl.BlockSpec((tok, BLK), lambda h: (0, 2 * pairs + h)),
            pl.BlockSpec((2, tok, tok), lambda h: (h, 0, 0)),
            pl.BlockSpec((tok, BLK), lambda h: (0, h)),
            pl.BlockSpec((tok, BLK), lambda h: (0, h)),
        ],
        out_specs=[
            pl.BlockSpec((tok, width), lambda h: (0, 0)),
            pl.BlockSpec((2, 5, BLK, BLK), lambda h: (h, 0, 0, 0)),
        ],
        out_shape=[
            jax.ShapeDtypeStruct((tok, width), BF16),
            jax.ShapeDtypeStruct((2 * pairs, 5, BLK, BLK), BF16),
        ],
        scratch_shapes=[pltpu.VMEM((tok, tok), BF16)],
        compiler_params=pltpu.CompilerParams(vmem_limit_bytes=40 * 1024 * 1024),
        cost_estimate=pl.CostEstimate(
            flops=20 * tok * tok * heads_w,
            bytes_accessed=12 * tok * width + 4 * pairs * tok * tok,
            transcendentals=0,
        ),
        name="attn_bwd",
    )(qkv, qkv, qkv, p, do, o)


def rep_index(x, yh, z):
    return ((x % NX) * NY + yh % NY) * NZ + z % NZ


def rep_shift(dx, dy, dz):
    return [
        (rep_index(x, y, z), rep_index(x + dx, y + dy, z + dz))
        for x in range(NX)
        for y in range(NY)
        for z in range(NZ)
    ]


def y_shift(dy, flip):
    reps = NX * NY * NZ
    pairs = []
    for x in range(NX):
        for yh in range(NY):
            for z in range(NZ):
                for yl in range(2):
                    for core in range(2):
                        y = (yh * 2 + yl + dy) % 4
                        source = (yl * 2 + core) * reps + rep_index(x, yh, z)
                        target = ((y % 2) * 2 + (core ^ flip)) * reps + rep_index(x, y // 2, z)
                        pairs.append((source, target))
    return pairs


def swap(value, bits):
    return lax.ppermute(value, "shard", [(s, s ^ bits) for s in range(4)])


def along_y(value, dy, flip):
    return lax.ppermute(value, ("shard", "rep"), y_shift(dy, flip))


def spread(value):
    near = swap(value, 1)
    far = swap(value, 2)
    return (value, near, far, swap(far, 1))


def in_order(values, me):
    a, b, c, d = values
    odd = (me & 1) == 1
    a, b = jnp.where(odd, b, a), jnp.where(odd, a, b)
    c, d = jnp.where(odd, d, c), jnp.where(odd, c, d)
    high = (me & 2) == 2
    return jnp.concatenate(
        [
            jnp.where(high, c, a),
            jnp.where(high, d, b),
            jnp.where(high, a, c),
            jnp.where(high, b, d),
        ],
        0,
    )


def take(array, index):
    return lax.dynamic_index_in_dim(array, index, 0, keepdims=False)


def exchange_sum(array, here, size, shift):
    total = take(array, here).astype(F32)
    for step in range(1, size):
        sent = take(array, (here + step) % size)
        total = total + lax.ppermute(sent, "rep", shift(step)).astype(F32)
    return total


def x_sum(array, x):
    return exchange_sum(array, x, NX, lambda s: rep_shift(s, 0, 0))


def z_sum(array, z):
    return exchange_sum(array, z, NZ, lambda s: rep_shift(0, 0, s))


def y_sum(array, y):
    return exchange_sum(array, y, NY, lambda s: rep_shift(0, s, 0))


def scatter_xzy(array, place):
    x, y, z = place
    rest = array.shape[1:]
    part = x_sum(array.reshape((NX, NY, NZ) + rest), x).astype(BF16)
    part = z_sum(jnp.swapaxes(part, 0, 1), z).astype(BF16)
    return y_sum(part, y)


def scatter_zxy(array, place):
    x, y, z = place
    rest = array.shape[1:]
    part = array.reshape((NX, NY, NZ) + rest)
    part = z_sum(jnp.moveaxis(part, 2, 0), z).astype(BF16)
    part = x_sum(part, x).astype(BF16)
    return y_sum(part, y)


def on_device(
    tokens,
    lengths,
    routes,
    attn_in,
    attn_proj,
    norm_first,
    norm_second,
    rel_bias,
    router,
    expert_in,
    expert_out,
    cotangent,
):
    me = lax.axis_index("shard")
    rep = lax.axis_index("rep")
    place = (rep // (NY * NZ), (rep // NZ) % NY, rep % NZ)
    core = me & 1
    odd = core == 1
    levels, own_rows, width3 = attn_in.shape
    width = width3 // 3
    half = width // 2
    tok = 4 * BLK
    heads = rel_bias.shape[2]
    heads_own = heads // 2
    buckets = rel_bias.shape[1]
    experts = router.shape[2]
    cap = BLK // 2

    def column_halves(block):
        parts = [block[..., i * half : (i + 1) * half] for i in range(6)]
        low = jnp.concatenate(parts[0::2], -1)
        high = jnp.concatenate(parts[1::2], -1)
        return jnp.where(odd, high, low), jnp.where(odd, low, high)

    mine, others = column_halves(attn_in)
    cut = own_rows // 2

    def gather_qkv(level, mine, others):
        near = swap(others, 1)
        same = jnp.concatenate(
            [along_y(mine[:cut], 1, 0), along_y(mine[cut:], -1, 0)], 0
        )
        cross = jnp.concatenate(
            [along_y(others[:cut], 1, 1), along_y(others[cut:], -1, 1)], 0
        )
        return in_order((mine, near, same, cross), me)

    token_parts = spread(tokens[0])
    route_parts = (routes[0], swap(routes[0], 1), swap(routes[0], 2), swap(routes[0], 3))
    w_qkv0 = gather_qkv(0, mine[0], others[0])
    x0 = in_order(token_parts, me)
    w_qkv0, x0, proj_own, mine1, others1, cot_own = lax.optimization_barrier(
        (w_qkv0, x0, attn_proj, mine[1], others[1], cotangent[0])
    )
    far = jnp.concatenate(
        [along_y(proj_own[:, :cut], 1, 0), along_y(proj_own[:, cut:], -1, 0)], 1
    )
    proj_parts = (proj_own, swap(proj_own, 1), far, swap(far, 1))
    w_proj = [in_order([part[level] for part in proj_parts], me) for level in range(levels)]
    w_qkv = [w_qkv0, gather_qkv(1, mine1, others1)]
    cot = in_order(spread(cot_own), me).astype(F32)

    position = jnp.arange(tok, dtype=jnp.int32)
    ends = jnp.cumsum(lengths[0])
    doc = jnp.sum((position[:, None] >= ends[None, :]).astype(jnp.int32), -1).astype(F32)
    docq, dock = doc[:, None], doc[None, :]
    offset = (
        BLK * (jnp.arange(5, dtype=jnp.int32) - 2)[:, None, None]
        + jnp.arange(BLK, dtype=jnp.int32)[None, None, :]
        - jnp.arange(BLK, dtype=jnp.int32)[None, :, None]
    )
    bucket_id = bucket_of(offset)
    bucket_hot = bucket_id[None] == jnp.arange(buckets, dtype=jnp.int32)[:, None, None, None]
    own_bias = jnp.where(odd, rel_bias[:, :, heads_own:], rel_bias[:, :, :heads_own])
    bias_blocks = jnp.einsum(
        "lbh,bdij->lhdij", own_bias, bucket_hot.astype(F32), precision=HIGH
    )
    route = in_order([part[None] for part in route_parts], me)
    onehot = (route[..., None] == jnp.arange(experts, dtype=jnp.int32)).astype(jnp.int32)
    slot = jnp.sum(jnp.cumsum(onehot, axis=1) * onehot, -1) - 1
    dispatch = (
        (route == me)[:, None, :] & (slot[:, None, :] == jnp.arange(cap)[None, :, None])
    ).astype(BF16)
    at_slot = jnp.arange(4, dtype=jnp.int32)[:, None] * cap + slot
    collect = [
        (
            (route.reshape(tok) == (me ^ r))[:, None]
            & (at_slot.reshape(tok)[:, None] == jnp.arange(4 * cap)[None, :])
        ).astype(BF16)
        for r in range(4)
    ]
    chosen = onehot.reshape(tok, experts).astype(F32)

    def rows_of(stream):
        return jnp.einsum(
            "bct,btd->bcd", dispatch, stream.reshape(4, BLK, -1), preferred_element_type=F32
        ).reshape(4 * cap, -1)

    def gathered(parts):
        return (
            dot(collect[0], parts[0])
            + dot(collect[1], parts[1])
            + dot(collect[2], parts[2])
            + dot(collect[3], parts[3])
        )

    def cols_of(array):
        return lax.dynamic_slice_in_dim(array, me * own_rows, own_rows, 1)

    saved = []
    stream = x0.astype(F32)
    for level in range(levels):
        normed = rms_norm(stream, norm_first[level]).astype(BF16)
        qkv = dot(normed, w_qkv[level]).astype(BF16)
        o_own, probs = attn_fwd(qkv, bias_blocks[level], docq, dock)
        o_near = swap(o_own, 1)
        mixed = jnp.concatenate(
            [jnp.where(odd, o_near, o_own), jnp.where(odd, o_own, o_near)], 1
        )
        after = stream + dot(mixed, w_proj[level])
        normed_two = rms_norm(after, norm_second[level]).astype(BF16)
        logits = dot(normed_two, router[level])
        route_probs = jax.nn.softmax(logits, -1)
        gate = jnp.sum(route_probs * chosen, -1)
        rows = rows_of(normed_two).astype(BF16)
        hidden = dot(rows, expert_in[level, 0])
        active = gelu_tanh(hidden).astype(BF16)
        made = dot(active, expert_out[level, 0]).astype(BF16)
        saved.append(
            (stream, normed, qkv, o_own, probs, mixed, after, normed_two, route_probs, gate,
             rows, hidden, active, made)
        )
        if level < levels - 1:
            stream = after + gate[:, None] * gathered(spread(made))

    blocks = made.reshape(4, cap, width)
    home = [take(blocks, me)] + [swap(take(blocks, me ^ r), r) for r in (1, 2, 3)]
    own_route, own_slot = take(route, me), take(slot, me)
    back = sum(
        dot(
            (
                (own_route == (me ^ r))[:, None]
                & (own_slot[:, None] == jnp.arange(cap)[None, :])
            ).astype(BF16),
            home[r],
        )
        for r in range(4)
    )
    own_gate = lax.dynamic_slice_in_dim(gate, me * BLK, BLK, 0)
    own_after = lax.dynamic_slice_in_dim(after, me * BLK, BLK, 0)
    result = (own_after + own_gate[:, None] * back).astype(BF16)[None]

    upstream = cot
    packs = [None] * levels
    inner_parts = [None] * levels
    outer_parts = [None] * levels
    for level in reversed(range(levels)):
        (stream, normed, qkv, o_own, probs, mixed, after, normed_two, route_probs, gate,
         rows, hidden, active, made) = saved[level]
        w_inner, w_outer = expert_in[level, 0], expert_out[level, 0]
        made_grad = rows_of((gate[:, None] * upstream).astype(BF16)).astype(BF16)
        active_grad = dot(made_grad, w_outer, ((1,), (1,)))
        _, gelu_pull = jax.vjp(gelu_tanh, hidden)
        hidden_grad = gelu_pull(active_grad)[0].astype(BF16)
        gate_grad = jnp.sum(made_grad.astype(F32) * made.astype(F32), -1)
        slot_probs = jnp.einsum(
            "bct,bte->bce", dispatch.astype(F32), route_probs.reshape(4, BLK, experts),
            precision=HIGH,
        ).reshape(4 * cap, experts)
        is_me = (jnp.arange(experts) == me).astype(F32)
        slot_logit_grad = gate_grad[:, None] * (is_me[None] - slot_probs)
        rows_grad = (
            dot(hidden_grad, w_inner, ((1,), (1,)))
            + dot(slot_logit_grad, router[level].astype(F32), ((1,), (1,)))
        ).astype(BF16)
        grads_home = spread(rows_grad)
        gate_home = (gate_grad, swap(gate_grad, 1), swap(gate_grad, 2), swap(gate_grad, 3))
        outer = dot(active, made_grad, ((0,), (0,))).astype(BF16)
        inner = dot(rows, hidden_grad, ((0,), (0,))).astype(BF16)
        inner_parts[level] = scatter_xzy(inner.reshape(32, width // 32, -1), place)
        outer_parts[level] = scatter_zxy(outer.reshape(32, outer.shape[0] // 32, -1), place)

        normed_grad = gathered(grads_home)
        token_gate_grad = sum(
            jnp.sum(collect[r].astype(F32) * gate_home[r][None], -1) for r in range(4)
        )
        logit_grad = token_gate_grad[:, None] * (chosen - route_probs)
        attn_side, grad_second = norm_back(after, norm_second[level], normed_grad)
        after_grad = upstream + attn_side
        branch_grad = after_grad.astype(BF16)
        w_proj_own = lax.dynamic_slice_in_dim(w_proj[level], core * half, half, 0)
        mixed_grad = dot(branch_grad, w_proj_own, ((1,), (1,))).astype(BF16)
        qkv_grad, bias_sums = attn_bwd(qkv, probs, mixed_grad, o_own)
        first_part = dot(qkv_grad, w_qkv[level], ((1,), (1,))).astype(BF16)
        first_grad = first_part.astype(F32) + swap(first_part, 1).astype(F32)
        input_side, grad_first = norm_back(stream, norm_first[level], first_grad)
        upstream = after_grad + input_side

        grad_proj = dot(cols_of(mixed), branch_grad, ((0,), (0,)))
        near_cols = lax.dynamic_slice_in_dim(normed, (me ^ 1) * own_rows, own_rows, 1)
        grad_qkv_own = dot(cols_of(normed), qkv_grad, ((0,), (0,))).astype(BF16)
        grad_qkv_near = swap(dot(near_cols, qkv_grad, ((0,), (0,))).astype(BF16), 1)
        pieces = []
        for part in range(3):
            a = grad_qkv_own[:, part * half : (part + 1) * half]
            b = grad_qkv_near[:, part * half : (part + 1) * half]
            pieces += [jnp.where(odd, b, a), jnp.where(odd, a, b)]
        bias_own = jnp.einsum(
            "hdij,bdij->bh", bias_sums, bucket_hot.astype(BF16), preferred_element_type=F32
        )
        bias_near = swap(bias_own, 1)
        grad_bias = jnp.concatenate(
            [jnp.where(odd, bias_near, bias_own), jnp.where(odd, bias_own, bias_near)], 1
        )
        grad_bias = lax.dynamic_slice_in_dim(
            grad_bias.reshape(-1), me * (buckets * heads // 4), buckets * heads // 4, 0
        )
        grad_router = dot(
            cols_of(normed_two).astype(F32), logit_grad, ((0,), (0,))
        )
        own_vec = lambda vec: lax.dynamic_slice_in_dim(vec, me * own_rows, own_rows, 0)
        small = jnp.concatenate(
            [
                own_vec(grad_first).reshape(32, -1),
                own_vec(grad_second).reshape(32, -1),
                grad_bias.reshape(32, -1),
                grad_router.reshape(32, -1),
            ],
            1,
        )
        small = jnp.pad(small, ((0, 0), (0, BLK - small.shape[1]))).astype(BF16)
        table = jnp.concatenate(pieces + [grad_proj.astype(BF16)], 1)
        packs[level] = (table.reshape(32, own_rows // 32, -1), small)

    per = own_rows // 32
    outs = []
    for level in range(levels):
        table, small = packs[level]
        flat = jnp.concatenate([table.reshape(32, -1), small], 1)
        summed = scatter_xzy(flat, place)
        big = summed[: per * 4 * width].reshape(per, 4 * width)
        tiny = summed[per * 4 * width :]
        outs.append(
            (
                big[:, :width3],
                big[:, width3:],
                tiny[:per],
                tiny[per : 2 * per],
                tiny[2 * per : 2 * per + buckets * heads // 128],
                tiny[2 * per + buckets * heads // 128 :][: per * experts].reshape(per, experts),
            )
        )
    stacked = [jnp.stack(items, 0) for items in zip(*outs)]
    expert_in_grad = jnp.stack(inner_parts, 0)[:, None]
    expert_out_grad = jnp.stack(outer_parts, 0)[:, None]
    own_up = lax.dynamic_slice_in_dim(upstream, me * BLK, BLK, 0)
    tokens_grad = own_up.astype(BF16)[None]
    return (result, tokens_grad, *stacked, expert_in_grad, expert_out_grad)


def solution(mesh):
    return jax.shard_map(
        on_device,
        mesh=mesh,
        in_specs=(
            P("rep", "shard", None),
            P("rep", None),
            P("rep", "shard"),
            P(None, "shard", None),
            P(None, "shard", None),
            P(),
            P(),
            P(),
            P(),
            P(None, "shard", None, None),
            P(None, "shard", None, None),
            P("rep", "shard", None),
        ),
        out_specs=(
            P("rep", "shard", None),
            P("rep", "shard", None),
            P(None, ("shard", "rep"), None),
            P(None, ("shard", "rep"), None),
            P(None, ("shard", "rep")),
            P(None, ("shard", "rep")),
            P(None, ("shard", "rep")),
            P(None, ("shard", "rep"), None),
            P(None, "shard", "rep", None),
            P(None, "shard", "rep", None),
        ),
        check_vma=False,
    )
```

```python
import functools

import jax
import jax.numpy as jnp
from jax import lax
from jax.experimental import pallas as pl
from jax.experimental.pallas import tpu as pltpu
from jax.sharding import PartitionSpec as P

EPS = 1e-06
SCALE = 0.125
NEG = -1e30
THRESHOLDS = (12, 16, 23, 32, 46, 64, 91)
HIGH = lax.Precision.HIGHEST
F32 = jnp.float32
BF16 = jnp.bfloat16
BRIEF = pl.CostEstimate(flops=10**6, bytes_accessed=10**5, transcendentals=0)
BLK = 128
NX, NY, NZ = 4, 2, 4


def bucket_of(offset):
    distance = jnp.abs(offset)
    far_bucket = 8 + sum(((distance >= threshold).astype(jnp.int32) for threshold in THRESHOLDS))
    bucket_id = jnp.where(distance < 8, distance, far_bucket)
    return bucket_id + 16 * (offset > 0).astype(jnp.int32)


def rms_norm(vector, gain_vec):
    inverse = lax.rsqrt(jnp.mean(vector * vector, -1, keepdims=True) + EPS)
    return vector * inverse * gain_vec


def norm_back(vector, gain_vec, upstream):
    inverse = lax.rsqrt(jnp.mean(vector * vector, -1, keepdims=True) + EPS)
    scaled = upstream * gain_vec
    grad_gain = jnp.sum(upstream * vector * inverse, 0)
    grad_in = inverse * scaled - vector * (inverse * inverse * inverse) * jnp.mean(
        scaled * vector, -1, keepdims=True
    )
    return (grad_in, grad_gain)


def gelu_tanh(vector):
    return jax.nn.gelu(vector, approximate=True)


def dot(a, b, dims=((1,), (0,))):
    return lax.dot_general(a, b, (dims, ((), ())), preferred_element_type=F32)


def attn_fwd_kernel(q_ref, k_ref, v_ref, line_ref, docq_ref, dock_ref, o_ref, p_ref):
    tok = q_ref.shape[0]
    nblk = tok // BLK
    first = lax.broadcasted_iota(jnp.int32, (1, BLK), 1) < BLK // 2
    k = k_ref[...]
    v = v_ref[...]
    bias = []
    for hh in range(2):
        blocks = []
        for d in range(5):
            line = jnp.broadcast_to(line_ref[0, hh, d : d + 1, :], (BLK, 2 * BLK))
            if d in (1, 2, 3):
                line = pltpu.roll(line, 0, 1, stride=1, stride_axis=0)
            blocks.append(line[:, :BLK])
        bias.append(blocks)
    for i in range(nblk):
        rows = slice(i * BLK, (i + 1) * BLK)
        same = docq_ref[rows, :] == dock_ref[...]
        q = q_ref[rows, :]
        outs = []
        for hh in range(2):
            mine = first if hh == 0 else jnp.logical_not(first)
            qm = jnp.where(mine, q, jnp.zeros_like(q))
            s = dot(qm, k, ((1,), (1,))) * SCALE
            spread_bias = jnp.concatenate(
                [bias[hh][max(-2, min(2, j - i)) + 2] for j in range(nblk)], axis=1
            )
            s = jnp.where(same, s + spread_bias, NEG)
            e = jnp.exp(s - jnp.max(s, -1, keepdims=True))
            p = (e * (1.0 / jnp.sum(e, -1, keepdims=True))).astype(BF16)
            p_ref[hh, rows, :] = p
            outs.append(dot(p, v))
        o_ref[rows, :] = jnp.where(first, outs[0], outs[1]).astype(BF16)


def attn_fwd(qkv, lines, docq, dock):
    tok, width = qkv.shape
    heads_w = width // 3
    pairs = heads_w // BLK
    return pl.pallas_call(
        attn_fwd_kernel,
        grid=(pairs,),
        in_specs=[
            pl.BlockSpec((tok, BLK), lambda h: (0, h)),
            pl.BlockSpec((tok, BLK), lambda h: (0, pairs + h)),
            pl.BlockSpec((tok, BLK), lambda h: (0, 2 * pairs + h)),
            pl.BlockSpec((1, 2, 8, 2 * BLK), lambda h: (h, 0, 0, 0)),
            pl.BlockSpec((tok, 1), lambda h: (0, 0)),
            pl.BlockSpec((1, tok), lambda h: (0, 0)),
        ],
        out_specs=[
            pl.BlockSpec((tok, BLK), lambda h: (0, h)),
            pl.BlockSpec((2, tok, tok), lambda h: (h, 0, 0)),
        ],
        out_shape=[
            jax.ShapeDtypeStruct((tok, heads_w), BF16),
            jax.ShapeDtypeStruct((2 * pairs, tok, tok), BF16),
        ],
        compiler_params=pltpu.CompilerParams(vmem_limit_bytes=40 * 1024 * 1024),
        cost_estimate=BRIEF,
        name="attn_fwd",
    )(qkv, qkv, qkv, lines, docq, dock)


def attn_bwd_kernel(q_ref, k_ref, v_ref, p_ref, do_ref, o_ref, dqkv_ref, m_ref, ds_ref):
    tok = q_ref.shape[0]
    nblk = tok // BLK
    pairs = pl.num_programs(0)
    step = pl.program_id(0)
    first = lax.broadcasted_iota(jnp.int32, (1, BLK), 1) < BLK // 2
    k = k_ref[...]
    v = v_ref[...]
    q = q_ref[...]
    do = do_ref[...]
    dk = jnp.zeros((tok, BLK), F32)
    dv = jnp.zeros((tok, BLK), F32)
    dqs = []
    for hh in range(2):
        mine = first if hh == 0 else jnp.logical_not(first)
        dom = jnp.where(mine, do, jnp.zeros_like(do))
        qm = jnp.where(mine, q, jnp.zeros_like(q))
        parts = [None] * 5
        dq_rows = []
        for i in range(nblk):
            rows = slice(i * BLK, (i + 1) * BLK)
            doi = dom[rows, :]
            dp = dot(doi, v, ((1,), (1,)))
            base = jnp.sum(
                doi.astype(F32) * o_ref[rows, :].astype(F32), -1, keepdims=True
            )
            ds = p_ref[hh, rows, :].astype(F32) * (dp - base)
            for j in range(nblk):
                d = max(-2, min(2, j - i)) + 2
                piece = ds[:, j * BLK : (j + 1) * BLK]
                parts[d] = piece if parts[d] is None else parts[d] + piece
            dsb = ds.astype(BF16)
            ds_ref[rows, :] = dsb
            dq_rows.append(dot(dsb, k))
        for d in range(5):
            m_ref[hh, d] = parts[d].astype(BF16)
        dqs.append(dq_rows)
        dk = dk + dot(ds_ref[...], qm, ((0,), (0,)))
        dv = dv + dot(p_ref[hh], dom, ((0,), (0,)))
    at = lambda part: pl.ds(pl.multiple_of((part * pairs + step) * BLK, BLK), BLK)
    for i in range(nblk):
        rows = slice(i * BLK, (i + 1) * BLK)
        dqkv_ref[rows, at(0)] = (jnp.where(first, dqs[0][i], dqs[1][i]) * SCALE).astype(BF16)
    dqkv_ref[:, at(1)] = (dk * SCALE).astype(BF16)
    dqkv_ref[:, at(2)] = dv.astype(BF16)


def attn_bwd(qkv, p, do, o):
    tok, width = qkv.shape
    heads_w = width // 3
    pairs = heads_w // BLK
    return pl.pallas_call(
        attn_bwd_kernel,
        grid=(pairs,),
        in_specs=[
            pl.BlockSpec((tok, BLK), lambda h: (0, h)),
            pl.BlockSpec((tok, BLK), lambda h: (0, pairs + h)),
            pl.BlockSpec((tok, BLK), lambda h: (0, 2 * pairs + h)),
            pl.BlockSpec((2, tok, tok), lambda h: (h, 0, 0)),
            pl.BlockSpec((tok, BLK), lambda h: (0, h)),
            pl.BlockSpec((tok, BLK), lambda h: (0, h)),
        ],
        out_specs=[
            pl.BlockSpec((tok, width), lambda h: (0, 0)),
            pl.BlockSpec((2, 5, BLK, BLK), lambda h: (h, 0, 0, 0)),
        ],
        out_shape=[
            jax.ShapeDtypeStruct((tok, width), BF16),
            jax.ShapeDtypeStruct((2 * pairs, 5, BLK, BLK), BF16),
        ],
        scratch_shapes=[pltpu.VMEM((tok, tok), BF16)],
        compiler_params=pltpu.CompilerParams(vmem_limit_bytes=40 * 1024 * 1024),
        cost_estimate=BRIEF,
        name="attn_bwd",
    )(qkv, qkv, qkv, p, do, o)


FCUT = 768


def gelu_both(u):
    c = 0.7978845608028654
    square = u * u
    t = jnp.tanh(c * u * (1.0 + 0.044715 * square))
    half = 0.5 * (1.0 + t)
    slope = half + 0.5 * c * u * (1.0 - t * t) * (1.0 + 3 * 0.044715 * square)
    return u * half, slope


def ffn_fwd_kernel(rows_ref, win_ref, wout_ref, made_ref, sum_ref):
    step = pl.program_id(0)
    act = gelu_both(dot(rows_ref[...], win_ref[...]))[0].astype(BF16)
    part = dot(act, wout_ref[...])

    @pl.when(step == 0)
    def _():
        sum_ref[...] = part

    @pl.when(step > 0)
    def _():
        sum_ref[...] += part

    @pl.when(step == pl.num_programs(0) - 1)
    def _():
        made_ref[...] = sum_ref[...].astype(BF16)


def ffn_fwd(rows, w_in, w_out, level):
    count, width = rows.shape
    ff = w_in.shape[-1]
    whole = pl.BlockSpec((count, width), lambda i: (0, 0))
    return pl.pallas_call(
        ffn_fwd_kernel,
        grid=(ff // FCUT,),
        in_specs=[
            whole,
            pl.BlockSpec((None, None, width, FCUT), lambda i: (level, 0, 0, i)),
            pl.BlockSpec((None, None, FCUT, width), lambda i: (level, 0, i, 0)),
        ],
        out_specs=whole,
        out_shape=jax.ShapeDtypeStruct((count, width), BF16),
        scratch_shapes=[pltpu.VMEM((count, width), F32)],
        compiler_params=pltpu.CompilerParams(vmem_limit_bytes=40 * 1024 * 1024),
        cost_estimate=BRIEF,
        name="ffn_fwd",
    )(rows, w_in, w_out)


def ffn_both_kernel(
    rows_ref, dy_ref, miss_ref, router_ref, win_ref, wout_ref,
    made_ref, msg_ref, gin_ref, gout_ref, sum_ref, dsum_ref,
):
    step = pl.program_id(0)
    rows = rows_ref[...]
    dy = dy_ref[...]
    act, slope = gelu_both(dot(rows, win_ref[...]))
    act = act.astype(BF16)
    part = dot(act, wout_ref[...])
    dhid = (dot(dy, wout_ref[...], ((1,), (1,))) * slope).astype(BF16)
    dpart = dot(dhid, win_ref[...], ((1,), (1,)))
    gin_ref[...] = dot(rows, dhid, ((0,), (0,))).astype(BF16)
    gout = dot(act, dy, ((0,), (0,))).astype(BF16)
    per = gout_ref.shape[2]
    for j in range(gout.shape[0] // per):
        gout_ref[j % NZ, j // NZ] = gout[j * per : (j + 1) * per]

    @pl.when(step == 0)
    def _():
        sum_ref[...] = part
        dsum_ref[...] = dpart

    @pl.when(step > 0)
    def _():
        sum_ref[...] += part
        dsum_ref[...] += dpart

    @pl.when(step == pl.num_programs(0) - 1)
    def _():
        count = rows_ref.shape[0]
        made = sum_ref[...].astype(BF16)
        made_ref[...] = made
        product = dy.astype(F32) * made.astype(F32)
        gate = jnp.sum(product, -1, keepdims=True)
        dlogits = (gate * miss_ref[...]).astype(BF16)
        msg_ref[:count, :] = (dsum_ref[...] + dot(dlogits, router_ref[...])).astype(BF16)
        ones = jnp.ones((16, product.shape[1]), F32)
        msg_ref[count:, :] = jnp.zeros((16, product.shape[1]), BF16)
        msg_ref[count:, :count] = dot(ones, product, ((1,), (1,))).astype(BF16)


def ffn_both(rows, dy, miss, router_t, w_in, w_out, level):
    count, width = rows.shape
    ff = w_in.shape[-1]
    per = ff // (NX * NY * NZ)
    whole = pl.BlockSpec((count, width), lambda i: (0, 0))
    return pl.pallas_call(
        ffn_both_kernel,
        grid=(ff // FCUT,),
        in_specs=[
            whole,
            whole,
            pl.BlockSpec(miss.shape, lambda i: (0, 0)),
            pl.BlockSpec(router_t.shape, lambda i: (0, 0)),
            pl.BlockSpec((None, None, width, FCUT), lambda i: (level, 0, 0, i)),
            pl.BlockSpec((None, None, FCUT, width), lambda i: (level, 0, i, 0)),
        ],
        out_specs=[
            whole,
            pl.BlockSpec((count + 16, width), lambda i: (0, 0)),
            pl.BlockSpec((width, FCUT), lambda i: (0, i)),
            pl.BlockSpec((NZ, FCUT // per // NZ, per, width), lambda i: (0, i, 0, 0)),
        ],
        out_shape=[
            jax.ShapeDtypeStruct((count, width), BF16),
            jax.ShapeDtypeStruct((count + 16, width), BF16),
            jax.ShapeDtypeStruct((width, ff), BF16),
            jax.ShapeDtypeStruct((NZ, NX * NY, per, width), BF16),
        ],
        scratch_shapes=[pltpu.VMEM((count, width), F32), pltpu.VMEM((count, width), F32)],
        compiler_params=pltpu.CompilerParams(vmem_limit_bytes=48 * 1024 * 1024),
        cost_estimate=BRIEF,
        name="ffn_both",
    )(rows, dy, miss, router_t, w_in, w_out)


def norm_back_block(vector, gain, upstream):
    inverse = lax.rsqrt(jnp.mean(vector * vector, -1, keepdims=True) + EPS)
    scaled = upstream * gain
    grad_gain = jnp.sum(upstream * vector * inverse, 0, keepdims=True)
    grad_in = inverse * scaled - vector * (inverse * inverse * inverse) * jnp.mean(
        scaled * vector, -1, keepdims=True
    )
    return grad_in, grad_gain


def add_up(ref, value):
    @pl.when(pl.program_id(0) == 0)
    def _():
        ref[...] = value

    @pl.when(pl.program_id(0) > 0)
    def _():
        ref[...] += value


def middle_bwd_kernel(
    place_ref, m0_ref, m1_ref, m2_ref, m3_ref, middle_ref, up_ref, gain_ref, proj_ref,
    grad_ref, branch_ref, mixed_ref, gain_grad_ref,
):
    count = place_ref.shape[0]
    rows = jnp.concatenate([m0_ref[...], m1_ref[...], m2_ref[...], m3_ref[...]], 0)
    hot = place_ref[...] == lax.broadcasted_iota(jnp.int32, (count, rows.shape[0]), 1)
    normed_grad = dot(hot.astype(F32).astype(BF16), rows)
    grad, gain_grad = norm_back_block(middle_ref[...], gain_ref[...], normed_grad)
    grad = up_ref[...].astype(F32) + grad
    grad_ref[...] = grad
    branch = grad.astype(BF16)
    branch_ref[...] = branch
    mixed_ref[...] = dot(branch, proj_ref[...], ((1,), (1,))).astype(BF16)
    add_up(gain_grad_ref, gain_grad)


def middle_bwd(place, parts, middle, up, gain, proj):
    tok, width = middle.shape
    half = proj.shape[0]
    cap = BLK // 2
    whole = lambda i: (0, 0)
    block = lambda i: (i, 0)
    return pl.pallas_call(
        middle_bwd_kernel,
        grid=(tok // BLK,),
        in_specs=[pl.BlockSpec((BLK, 1), block)]
        + [pl.BlockSpec((cap, width), block)] * 4
        + [
            pl.BlockSpec((BLK, width), block),
            pl.BlockSpec((BLK, width), block),
            pl.BlockSpec((1, width), whole),
            pl.BlockSpec((half, width), whole),
        ],
        out_specs=[
            pl.BlockSpec((BLK, width), block),
            pl.BlockSpec((BLK, width), block),
            pl.BlockSpec((BLK, half), block),
            pl.BlockSpec((1, width), whole),
        ],
        out_shape=[
            jax.ShapeDtypeStruct((tok, width), F32),
            jax.ShapeDtypeStruct((tok, width), BF16),
            jax.ShapeDtypeStruct((tok, half), BF16),
            jax.ShapeDtypeStruct((1, width), F32),
        ],
        compiler_params=pltpu.CompilerParams(vmem_limit_bytes=32 * 1024 * 1024),
        cost_estimate=BRIEF,
        name="middle_bwd",
    )(place, *parts, middle, up, gain[None], proj)


def first_bwd_kernel(
    place_ref, own_ref, near_ref, stream_ref, grad_ref, gain_ref, gate_ref,
    up_ref, made_ref, gain_grad_ref,
):
    count = place_ref.shape[0]
    first_grad = own_ref[...].astype(F32) + near_ref[...].astype(F32)
    grad, gain_grad = norm_back_block(stream_ref[...], gain_ref[...], first_grad)
    grad = grad_ref[...] + grad
    up_ref[...] = grad
    hot = place_ref[...] == lax.broadcasted_iota(jnp.int32, (count, BLK), 1)
    gated = (gate_ref[...] * grad).astype(BF16)
    made = dot(hot.astype(F32).astype(BF16), gated, ((0,), (0,)))
    made_ref[...] = made[: made_ref.shape[0]].astype(BF16)
    add_up(gain_grad_ref, gain_grad)


def first_bwd(place, own, near, stream, grad, gain, gate):
    tok, width = stream.shape
    cap = BLK // 2
    whole = lambda i: (0, 0)
    block = lambda i: (i, 0)
    wide = pl.BlockSpec((BLK, width), block)
    return pl.pallas_call(
        first_bwd_kernel,
        grid=(tok // BLK,),
        in_specs=[
            pl.BlockSpec((BLK, 1), block), wide, wide, wide, wide,
            pl.BlockSpec((1, width), whole), pl.BlockSpec((BLK, 1), block),
        ],
        out_specs=[wide, pl.BlockSpec((cap, width), block), pl.BlockSpec((1, width), whole)],
        out_shape=[
            jax.ShapeDtypeStruct((tok, width), F32),
            jax.ShapeDtypeStruct((tok // 2, width), BF16),
            jax.ShapeDtypeStruct((1, width), F32),
        ],
        compiler_params=pltpu.CompilerParams(vmem_limit_bytes=32 * 1024 * 1024),
        cost_estimate=BRIEF,
        name="first_bwd",
    )(place, own, near, stream, grad, gain[None], gate)


def rep_index(x, yh, z):
    return ((x % NX) * NY + yh % NY) * NZ + z % NZ


def rep_shift(dx, dy, dz):
    return [
        (rep_index(x, y, z), rep_index(x + dx, y + dy, z + dz))
        for x in range(NX)
        for y in range(NY)
        for z in range(NZ)
    ]


def y_shift(dy, flip):
    reps = NX * NY * NZ
    pairs = []
    for x in range(NX):
        for yh in range(NY):
            for z in range(NZ):
                for yl in range(2):
                    for core in range(2):
                        y = (yh * 2 + yl + dy) % 4
                        source = (yl * 2 + core) * reps + rep_index(x, yh, z)
                        target = ((y % 2) * 2 + (core ^ flip)) * reps + rep_index(x, y // 2, z)
                        pairs.append((source, target))
    return pairs


def swap(value, bits):
    return lax.ppermute(value, "shard", [(s, s ^ bits) for s in range(4)])


def along_y(value, dy, flip):
    return lax.ppermute(value, ("shard", "rep"), y_shift(dy, flip))


def spread(value):
    near = swap(value, 1)
    far = swap(value, 2)
    return (value, near, far, swap(far, 1))


def in_order(values, me):
    rows = values[0].shape[0]
    whole = jnp.zeros((4 * rows,) + values[0].shape[1:], values[0].dtype)
    for r, value in enumerate(values):
        whole = lax.dynamic_update_slice_in_dim(whole, value, (me ^ r) * rows, 0)
    return whole


def take(array, index, axis=0):
    return lax.dynamic_index_in_dim(array, index, axis, keepdims=False)


def after(values, on):
    return lax.optimization_barrier((values, on))[0]


def exchange(array, axis, here, size, shift):
    got = [take(array, here, axis)]
    for step in range(1, size):
        got.append(lax.ppermute(take(array, (here + step) % size, axis), "rep", shift(step)))
    return got


def total(parts):
    return sum(part.astype(F32) for part in parts)


def x_parts(array, axis, place):
    return exchange(array, axis, place[0], NX, lambda s: rep_shift(s, 0, 0))


def y_parts(array, axis, place):
    return exchange(array, axis, place[1], NY, lambda s: rep_shift(0, s, 0))


def z_parts(array, axis, place):
    return exchange(array, axis, place[2], NZ, lambda s: rep_shift(0, 0, s))


def x_groups():
    return [[rep_index(x, y, z) for x in range(NX)] for y in range(NY) for z in range(NZ)]


def z_groups():
    return [[rep_index(x, y, z) for z in range(NZ)] for x in range(NX) for y in range(NY)]


def inner_first(inner):
    return lax.psum_scatter(
        inner, "rep", scatter_dimension=0, tiled=True, axis_index_groups=x_groups()
    )


def inner_y(part, place):
    return y_parts(part.reshape(NY, part.shape[0] // NY, part.shape[1]), 0, place)


def outer_first(outer):
    return lax.all_to_all(
        outer, "rep", split_axis=0, concat_axis=0, tiled=True, axis_index_groups=z_groups()
    )


def outer_sum(parts):
    return jnp.sum(parts.astype(F32), 0).astype(BF16)


def outer_y(parts, place):
    part = outer_sum(parts)
    return y_parts(part.reshape((NX, NY) + part.shape[1:]), 1, place)


def on_device(
    tokens,
    lengths,
    routes,
    attn_in,
    attn_proj,
    norm_first,
    norm_second,
    rel_bias,
    router,
    expert_in,
    expert_out,
    cotangent,
):
    me = lax.axis_index("shard")
    rep = lax.axis_index("rep")
    place = (rep // (NY * NZ), (rep // NZ) % NY, rep % NZ)
    core = me & 1
    odd = core == 1
    levels, own_rows, width3 = attn_in.shape
    width = width3 // 3
    half = width // 2
    tok = 4 * BLK
    heads = rel_bias.shape[2]
    heads_own = heads // 2
    buckets = rel_bias.shape[1]
    experts = router.shape[2]
    cap = BLK // 2

    def column_halves(block):
        parts = [block[..., i * half : (i + 1) * half] for i in range(6)]
        low = jnp.concatenate(parts[0::2], -1)
        high = jnp.concatenate(parts[1::2], -1)
        return jnp.where(odd, high, low), jnp.where(odd, low, high)

    cut = own_rows // 2
    route_row = jnp.zeros((16, width), BF16).at[0, :BLK].set(routes[0].astype(BF16))

    def fetch(own, axis):
        low = lax.slice_in_dim(own, 0, cut, axis=axis)
        high = lax.slice_in_dim(own, cut, 2 * cut, axis=axis)
        return along_y(low, 1, 0), along_y(high, -1, 0)

    def build_qkv(own, far):
        mine, others = column_halves(own)
        far_mine, far_others = column_halves(jnp.concatenate(far, 0))
        return in_order((mine, swap(others, 1), far_mine, swap(far_others, 1)), me)

    def build_proj(own, far):
        far = jnp.concatenate(far, 1)
        near = swap(jnp.stack([own, far], 0), 1)
        return [
            in_order((own[level], near[0, level], far[level], near[1, level]), me)
            for level in range(levels)
        ]

    w_qkv0 = build_qkv(attn_in[0], fetch(attn_in[0], 0))
    token_parts = spread(jnp.concatenate([tokens[0], route_row], 0))
    x0 = in_order([part[:BLK] for part in token_parts], me)
    route_parts = [part[BLK, :BLK].astype(jnp.int32) for part in token_parts]
    far_proj = fetch(after(attn_proj, w_qkv0), 1)

    position = jnp.arange(tok, dtype=jnp.int32)
    ends = jnp.cumsum(lengths[0])
    doc = jnp.sum((position[:, None] >= ends[None, :]).astype(jnp.int32), -1).astype(F32)
    docq, dock = doc[:, None], doc[None, :]
    own_bias = jnp.where(odd, rel_bias[:, :, heads_own:], rel_bias[:, :, :heads_own])
    turn = jnp.arange(2 * BLK, dtype=jnp.int32)
    line_offset = (
        BLK * (jnp.arange(8, dtype=jnp.int32) - 2)[:, None]
        + jnp.where(turn < BLK, turn, turn - 2 * BLK)[None]
    )
    line_hot = (
        bucket_of(line_offset)[None] == jnp.arange(buckets, dtype=jnp.int32)[:, None, None]
    ).astype(F32)
    lines = jnp.einsum("lbh,bdm->lhdm", own_bias, line_hot, precision=HIGH)
    lines = lines.reshape(levels, heads_own // 2, 2, 8, 2 * BLK)
    route = in_order([part[None] for part in route_parts], me)
    onehot = (route[..., None] == jnp.arange(experts, dtype=jnp.int32)).astype(jnp.int32)
    slot = jnp.sum(jnp.cumsum(onehot, axis=1) * onehot, -1) - 1
    dispatch = (
        (route == me)[:, None, :] & (slot[:, None, :] == jnp.arange(cap)[None, :, None])
    ).astype(BF16)
    at_slot = jnp.arange(4, dtype=jnp.int32)[:, None] * cap + slot
    collect = [
        (
            (route.reshape(tok) == (me ^ r))[:, None]
            & (at_slot.reshape(tok)[:, None] == jnp.arange(4 * cap)[None, :])
        ).astype(BF16)
        for r in range(4)
    ]
    chosen = onehot.reshape(tok, experts).astype(F32)
    spot = ((route ^ me) * cap + slot).reshape(tok, 1)

    router_ts = [
        jnp.pad(router[level].T, ((0, BLK - experts), (0, 0))) for level in range(levels)
    ]
    router_ts, spot, collect, chosen, x0 = lax.optimization_barrier(
        (router_ts, spot, collect, chosen, x0)
    )

    def rows_of(stream):
        return jnp.einsum(
            "bct,btd->bcd", dispatch, stream.reshape(4, BLK, -1), preferred_element_type=F32
        ).reshape(4 * cap, -1)

    def gathered(parts):
        return (
            dot(collect[0], parts[0])
            + dot(collect[1], parts[1])
            + dot(collect[2], parts[2])
            + dot(collect[3], parts[3])
        )

    def cols_of(array):
        return lax.dynamic_slice_in_dim(array, me * own_rows, own_rows, 1)

    saved = []
    misses = []
    w_qkv = [w_qkv0]
    stream = x0.astype(F32)
    for level in range(levels):
        normed = rms_norm(stream, norm_first[level]).astype(BF16)
        qkv = dot(normed, w_qkv[level]).astype(BF16)
        if level > 0:
            qkv, cot_own = lax.optimization_barrier((qkv, cotangent[0]))
            cot = in_order(spread(cot_own), me)
        o_own, probs = attn_fwd(qkv, lines[level], docq, dock)
        if level == 0:
            w_proj = build_proj(*after((attn_proj, far_proj), o_own))
            next_in = after(attn_in[1], o_own)
            next_far = fetch(next_in, 0)
        o_near = swap(o_own, 1)
        mixed = jnp.concatenate(
            [jnp.where(odd, o_near, o_own), jnp.where(odd, o_own, o_near)], 1
        )
        middle = stream + dot(mixed, w_proj[level])
        normed_two = rms_norm(middle, norm_second[level]).astype(BF16)
        logits = dot(normed_two, router[level])
        route_probs = jax.nn.softmax(logits, -1)
        gate = jnp.sum(route_probs * chosen, -1)
        rows = rows_of(normed_two).astype(BF16)
        slot_probs = jnp.einsum(
            "bct,bte->bce", dispatch, route_probs.reshape(4, BLK, experts).astype(BF16),
            preferred_element_type=F32,
        ).reshape(4 * cap, experts)
        miss = jnp.pad(
            (jnp.arange(experts) == me).astype(F32)[None] - slot_probs,
            ((0, 0), (0, BLK - experts)),
        )
        misses.append(miss)
        saved.append(
            (stream, normed, qkv, o_own, probs, mixed, middle, normed_two, route_probs, gate, rows)
        )
        if level < levels - 1:
            made = ffn_fwd(rows, expert_in, expert_out, level)
            w_qkv.append(build_qkv(*after((next_in, next_far), made)))
            made_parts = spread(made)
            w_proj_owns = [lax.dynamic_slice_in_dim(w, core * half, half, 0) for w in w_proj]
            middle, gate, misses, w_proj_owns, far_made = lax.optimization_barrier(
                (middle, gate, misses, w_proj_owns, made_parts[2])
            )
            made_parts = made_parts[:2] + (far_made,) + made_parts[3:]
            stream = middle + gate[:, None] * gathered(made_parts)

    def go_home(made, middle, gate):
        blocks = made.reshape(4, cap, width)
        home = [take(blocks, me)] + [swap(take(blocks, me ^ r), r) for r in (1, 2, 3)]
        own_route, own_slot = take(route, me), take(slot, me)
        back = sum(
            dot(
                (
                    (own_route == (me ^ r))[:, None]
                    & (own_slot[:, None] == jnp.arange(cap)[None, :])
                ).astype(BF16),
                home[r],
            )
            for r in range(4)
        )
        own_gate = lax.dynamic_slice_in_dim(gate, me * BLK, BLK, 0)
        own_after = lax.dynamic_slice_in_dim(middle, me * BLK, BLK, 0)
        result = (own_after + own_gate[:, None] * back).astype(BF16)[None]
        return result

    def pack(normed, mixed, normed_two, branch_grad, qkv_grad, bias_sums, message_parts,
             route_probs, grad_first, grad_second):
        chip_rows = lambda array, axis: lax.dynamic_slice_in_dim(
            array, (me >> 1) * 2 * own_rows, 2 * own_rows, axis
        )
        grad_qkv = dot(chip_rows(normed, 1), qkv_grad, ((0,), (0,))).astype(BF16)
        grad_proj = dot(cols_of(mixed), branch_grad, ((0,), (0,))).astype(BF16)
        token_gate_grad = sum(
            dot(collect[r], message_parts[r][4 * cap :, : 4 * cap], ((1,), (1,))) for r in range(4)
        )[:, :1]
        logit_grad = token_gate_grad * (chosen - route_probs)
        own_vec = lambda vec: lax.dynamic_slice_in_dim(vec, me * own_rows, own_rows, 0)[:, None]
        grad_router = dot(cols_of(normed_two), logit_grad.astype(BF16), ((0,), (0,)))
        own = jnp.concatenate([own_vec(grad_first), own_vec(grad_second), grad_router], 1)
        own = jnp.where(
            (jnp.arange(2) == core)[:, None, None], own[None], jnp.zeros_like(own)[None]
        )
        count = after(jnp.arange(BLK, dtype=jnp.int32), branch_grad)
        offset = (
            BLK * (jnp.arange(5, dtype=jnp.int32) - 2)[:, None, None]
            + count[None, None, :]
            - count[None, :, None]
        )
        bucket_id = bucket_of(offset)
        bucket_hot = bucket_id[None] == jnp.arange(buckets, dtype=jnp.int32)[:, None, None, None]
        bias_own = jnp.einsum(
            "hdij,bdij->bh", bias_sums, bucket_hot.astype(BF16), preferred_element_type=F32
        )
        none = jnp.zeros_like(bias_own)
        bias_all = jnp.where(
            odd,
            jnp.concatenate([none, bias_own], 1),
            jnp.concatenate([bias_own, none], 1),
        ).reshape(-1)
        bias_rows = lax.dynamic_slice_in_dim(
            bias_all, (me >> 1) * bias_all.shape[0] // 2, bias_all.shape[0] // 2, 0
        ).reshape(2, 32, -1)
        per = own_rows // 32
        bias_rows = jnp.pad(bias_rows, ((0, 0), (0, 0), (0, per - bias_rows.shape[2])))
        small = jnp.concatenate([own, bias_rows.reshape(2, own_rows, 1)], 2)
        small = jnp.pad(small, ((0, 0), (0, 0), (0, BLK - small.shape[2]))).astype(BF16)
        table = jnp.concatenate(
            [
                grad_qkv.reshape(2, own_rows, -1),
                jnp.stack([grad_proj[:, :half], grad_proj[:, half:]], 0),
                small,
            ],
            2,
        )
        table = table.reshape(2, NX, NY, NZ * per, table.shape[2])
        return table

    upstream = cot
    packs = [None] * levels
    inner_parts = [None] * levels
    outer_parts = [None] * levels
    for level in reversed(range(levels)):
        (stream, normed, qkv, o_own, probs, mixed, middle, normed_two, route_probs, gate,
         rows) = saved[level]
        if level == levels - 1:
            made_grad = rows_of((gate[:, None] * upstream.astype(F32)).astype(BF16)).astype(BF16)
        w_proj_own = w_proj_owns[level]
        made_grad, upstream, w_proj_own, spot = lax.optimization_barrier(
            (made_grad, upstream, w_proj_own, spot)
        )
        made, message, inner, outer = ffn_both(
            rows, made_grad, misses[level], router_ts[level], expert_in, expert_out, level
        )
        message_parts = spread(message)
        far_part = message_parts[2]
        if level == levels - 1:
            last = (made, middle, gate)
        inner, outer, upstream, middle, route_probs = after(
            (inner, outer, upstream, middle, route_probs), far_part
        )
        if level < levels - 1:
            over = level + 1
            inner_over, outer_over = after((inner_parts[over], outer_parts[over]), far_part)
            inner_parts[over] = inner_y(inner_over, place)
            outer_parts[over] = outer_y(outer_over, place)
            outer, _ = lax.optimization_barrier((outer, outer_over))
        inner_parts[level] = inner_first(inner)
        outer_parts[level] = outer_first(outer)
        after_grad, branch_grad, mixed_grad, grad_second = middle_bwd(
            spot, message_parts, middle, upstream, norm_second[level], w_proj_own
        )
        grad_second = grad_second[0]
        qkv_grad, bias_sums = attn_bwd(qkv, probs, mixed_grad, o_own)
        if level < levels - 1:
            pending, stream = after((pending, stream), qkv_grad)
            packs[level + 1] = pack(*pending)
        first_part = dot(qkv_grad, w_qkv[level], ((1,), (1,))).astype(BF16)
        near_first = swap(first_part, 1)
        if level > 0:
            upstream, made_grad, grad_first = first_bwd(
                spot, first_part, near_first, stream, after_grad, norm_first[level],
                saved[level - 1][9][:, None],
            )
            grad_first = grad_first[0]
        else:
            input_side, grad_first = norm_back(
                stream, norm_first[level], first_part.astype(F32) + near_first.astype(F32)
            )
            upstream = after_grad + input_side
        pending = (normed, mixed, normed_two, branch_grad, qkv_grad, bias_sums, message_parts,
                   route_probs, grad_first, grad_second)
        if level < levels - 1:
            packs[level] = pack(*pending)

    table = jnp.stack(packs, 0)
    outer_low, inner_low = after((outer_parts[0], inner_parts[0]), table)
    outer_low = outer_sum(outer_low)
    table = y_parts(table, 3, place)
    table, last = after((table, last), outer_low)
    result = go_home(*last)
    table = total(table).astype(BF16)
    table = total(x_parts(table, 2, place)).astype(BF16)
    per = own_rows // 32
    table = total(z_parts(table.reshape(levels, 2, NZ, per, -1), 2, place))
    inner_top = total(inner_parts[1]).astype(BF16)
    outer_top = total(outer_parts[1]).astype(BF16)
    rows_in = inner_low.shape[0] // (NY * NZ)
    inner_all = jnp.concatenate(
        [
            inner_low.reshape(NY, NZ, rows_in, -1),
            inner_top.reshape(1, NZ, rows_in, -1),
        ],
        0,
    )
    outer_all = jnp.concatenate(
        [outer_low.reshape((NX, NY) + outer_low.shape[1:]), outer_top[:, None]], 1
    )
    inner_all = total(z_parts(inner_all, 1, place))
    outer_all = total(x_parts(outer_all, 0, place))
    inner_low = total(y_parts(inner_all[:NY].astype(BF16), 0, place))
    outer_low = total(y_parts(outer_all[:NY].astype(BF16), 0, place))
    expert_in_grad = jnp.stack([inner_low, inner_all[NY]], 0)[:, None]
    expert_out_grad = jnp.stack([outer_low, outer_all[NY]], 0)[:, None]
    mine = take(table, core, 1)
    near = swap(take(table, core ^ 1, 1), 1)
    pieces = []
    for part in range(3):
        a = mine[..., part * half : (part + 1) * half]
        b = near[..., part * half : (part + 1) * half]
        pieces += [jnp.where(odd, b, a), jnp.where(odd, a, b)]
    attn_in_grad = jnp.concatenate(pieces, -1)
    at = width3 // 2
    attn_proj_grad = jnp.concatenate(
        [table[:, 0, :, at : at + half], table[:, 1, :, at : at + half]], -1
    )
    at += half
    few = buckets * heads // 128
    stacked = (
        attn_in_grad,
        attn_proj_grad,
        mine[:, :, at],
        mine[:, :, at + 1],
        mine[:, :few, at + 2 + experts] + near[:, :few, at + 2 + experts],
        mine[:, :, at + 2 : at + 2 + experts],
    )

    own_up = lax.dynamic_slice_in_dim(upstream, me * BLK, BLK, 0)
    tokens_grad = own_up.astype(BF16)[None]
    return (result, tokens_grad, *stacked, expert_in_grad, expert_out_grad)


def solution(mesh):
    return jax.shard_map(
        on_device,
        mesh=mesh,
        in_specs=(
            P("rep", "shard", None),
            P("rep", None),
            P("rep", "shard"),
            P(None, "shard", None),
            P(None, "shard", None),
            P(),
            P(),
            P(),
            P(),
            P(None, "shard", None, None),
            P(None, "shard", None, None),
            P("rep", "shard", None),
        ),
        out_specs=(
            P("rep", "shard", None),
            P("rep", "shard", None),
            P(None, ("shard", "rep"), None),
            P(None, ("shard", "rep"), None),
            P(None, ("shard", "rep")),
            P(None, ("shard", "rep")),
            P(None, ("shard", "rep")),
            P(None, ("shard", "rep"), None),
            P(None, "shard", "rep", None),
            P(None, "shard", "rep", None),
        ),
        check_vma=False,
    )
```

```python
import functools

import jax
import jax.numpy as jnp
from jax import lax
from jax.experimental import pallas as pl
from jax.experimental.pallas import tpu as pltpu
from jax.sharding import PartitionSpec as P

EPS = 1e-06
SCALE = 0.125
NEG = -1e30
THRESHOLDS = (12, 16, 23, 32, 46, 64, 91)
HIGH = lax.Precision.HIGHEST
F32 = jnp.float32
BF16 = jnp.bfloat16
BRIEF = pl.CostEstimate(flops=10**6, bytes_accessed=10**5, transcendentals=0)
BLK = 128
NX, NY, NZ = 4, 2, 4


def bucket_of(offset):
    distance = jnp.abs(offset)
    far_bucket = 8 + sum(((distance >= threshold).astype(jnp.int32) for threshold in THRESHOLDS))
    bucket_id = jnp.where(distance < 8, distance, far_bucket)
    return bucket_id + 16 * (offset > 0).astype(jnp.int32)


def rms_norm(vector, gain_vec):
    inverse = lax.rsqrt(jnp.mean(vector * vector, -1, keepdims=True) + EPS)
    return vector * inverse * gain_vec


def norm_back(vector, gain_vec, upstream):
    inverse = lax.rsqrt(jnp.mean(vector * vector, -1, keepdims=True) + EPS)
    scaled = upstream * gain_vec
    grad_gain = jnp.sum(upstream * vector * inverse, 0)
    grad_in = inverse * scaled - vector * (inverse * inverse * inverse) * jnp.mean(
        scaled * vector, -1, keepdims=True
    )
    return (grad_in, grad_gain)


def gelu_tanh(vector):
    return jax.nn.gelu(vector, approximate=True)


def dot(a, b, dims=((1,), (0,))):
    return lax.dot_general(a, b, (dims, ((), ())), preferred_element_type=F32)


def attn_fwd_kernel(q_ref, k_ref, v_ref, line_ref, docq_ref, dock_ref, o_ref, p_ref):
    tok = q_ref.shape[0]
    nblk = tok // BLK
    first = lax.broadcasted_iota(jnp.int32, (1, BLK), 1) < BLK // 2
    k = k_ref[...]
    v = v_ref[...]
    bias = []
    for hh in range(2):
        blocks = []
        for d in range(5):
            line = jnp.broadcast_to(line_ref[0, hh, d : d + 1, :], (BLK, 2 * BLK))
            if d in (1, 2, 3):
                line = pltpu.roll(line, 0, 1, stride=1, stride_axis=0)
            blocks.append(line[:, :BLK])
        bias.append(blocks)
    for i in range(nblk):
        rows = slice(i * BLK, (i + 1) * BLK)
        same = docq_ref[rows, :] == dock_ref[...]
        q = q_ref[rows, :]
        outs = []
        for hh in range(2):
            mine = first if hh == 0 else jnp.logical_not(first)
            qm = jnp.where(mine, q, jnp.zeros_like(q))
            s = dot(qm, k, ((1,), (1,))) * SCALE
            spread_bias = jnp.concatenate(
                [bias[hh][max(-2, min(2, j - i)) + 2] for j in range(nblk)], axis=1
            )
            s = jnp.where(same, s + spread_bias, NEG)
            e = jnp.exp(s - jnp.max(s, -1, keepdims=True))
            p = (e * (1.0 / jnp.sum(e, -1, keepdims=True))).astype(BF16)
            p_ref[hh, rows, :] = p
            outs.append(dot(p, v))
        o_ref[rows, :] = jnp.where(first, outs[0], outs[1]).astype(BF16)


def attn_fwd(qkv, lines, docq, dock):
    tok, width = qkv.shape
    heads_w = width // 3
    pairs = heads_w // BLK
    return pl.pallas_call(
        attn_fwd_kernel,
        grid=(pairs,),
        in_specs=[
            pl.BlockSpec((tok, BLK), lambda h: (0, h)),
            pl.BlockSpec((tok, BLK), lambda h: (0, pairs + h)),
            pl.BlockSpec((tok, BLK), lambda h: (0, 2 * pairs + h)),
            pl.BlockSpec((1, 2, 8, 2 * BLK), lambda h: (h, 0, 0, 0)),
            pl.BlockSpec((tok, 1), lambda h: (0, 0)),
            pl.BlockSpec((1, tok), lambda h: (0, 0)),
        ],
        out_specs=[
            pl.BlockSpec((tok, BLK), lambda h: (0, h)),
            pl.BlockSpec((2, tok, tok), lambda h: (h, 0, 0)),
        ],
        out_shape=[
            jax.ShapeDtypeStruct((tok, heads_w), BF16),
            jax.ShapeDtypeStruct((2 * pairs, tok, tok), BF16),
        ],
        compiler_params=pltpu.CompilerParams(vmem_limit_bytes=40 * 1024 * 1024),
        cost_estimate=BRIEF,
        name="attn_fwd",
    )(qkv, qkv, qkv, lines, docq, dock)


def attn_bwd_kernel(q_ref, k_ref, v_ref, p_ref, do_ref, o_ref, dqkv_ref, m_ref, ds_ref):
    tok = q_ref.shape[0]
    nblk = tok // BLK
    pairs = pl.num_programs(0)
    step = pl.program_id(0)
    first = lax.broadcasted_iota(jnp.int32, (1, BLK), 1) < BLK // 2
    k = k_ref[...]
    v = v_ref[...]
    q = q_ref[...]
    do = do_ref[...]
    dk = jnp.zeros((tok, BLK), F32)
    dv = jnp.zeros((tok, BLK), F32)
    dqs = []
    for hh in range(2):
        mine = first if hh == 0 else jnp.logical_not(first)
        dom = jnp.where(mine, do, jnp.zeros_like(do))
        qm = jnp.where(mine, q, jnp.zeros_like(q))
        parts = [None] * 5
        dq_rows = []
        for i in range(nblk):
            rows = slice(i * BLK, (i + 1) * BLK)
            doi = dom[rows, :]
            dp = dot(doi, v, ((1,), (1,)))
            base = jnp.sum(
                doi.astype(F32) * o_ref[rows, :].astype(F32), -1, keepdims=True
            )
            ds = p_ref[hh, rows, :].astype(F32) * (dp - base)
            for j in range(nblk):
                d = max(-2, min(2, j - i)) + 2
                piece = ds[:, j * BLK : (j + 1) * BLK]
                parts[d] = piece if parts[d] is None else parts[d] + piece
            dsb = ds.astype(BF16)
            ds_ref[rows, :] = dsb
            dq_rows.append(dot(dsb, k))
        for d in range(5):
            m_ref[hh, d] = parts[d].astype(BF16)
        dqs.append(dq_rows)
        dk = dk + dot(ds_ref[...], qm, ((0,), (0,)))
        dv = dv + dot(p_ref[hh], dom, ((0,), (0,)))
    at = lambda part: pl.ds(pl.multiple_of((part * pairs + step) * BLK, BLK), BLK)
    for i in range(nblk):
        rows = slice(i * BLK, (i + 1) * BLK)
        dqkv_ref[rows, at(0)] = (jnp.where(first, dqs[0][i], dqs[1][i]) * SCALE).astype(BF16)
    dqkv_ref[:, at(1)] = (dk * SCALE).astype(BF16)
    dqkv_ref[:, at(2)] = dv.astype(BF16)


def attn_bwd(qkv, p, do, o):
    tok, width = qkv.shape
    heads_w = width // 3
    pairs = heads_w // BLK
    return pl.pallas_call(
        attn_bwd_kernel,
        grid=(pairs,),
        in_specs=[
            pl.BlockSpec((tok, BLK), lambda h: (0, h)),
            pl.BlockSpec((tok, BLK), lambda h: (0, pairs + h)),
            pl.BlockSpec((tok, BLK), lambda h: (0, 2 * pairs + h)),
            pl.BlockSpec((2, tok, tok), lambda h: (h, 0, 0)),
            pl.BlockSpec((tok, BLK), lambda h: (0, h)),
            pl.BlockSpec((tok, BLK), lambda h: (0, h)),
        ],
        out_specs=[
            pl.BlockSpec((tok, width), lambda h: (0, 0)),
            pl.BlockSpec((2, 5, BLK, BLK), lambda h: (h, 0, 0, 0)),
        ],
        out_shape=[
            jax.ShapeDtypeStruct((tok, width), BF16),
            jax.ShapeDtypeStruct((2 * pairs, 5, BLK, BLK), BF16),
        ],
        scratch_shapes=[pltpu.VMEM((tok, tok), BF16)],
        compiler_params=pltpu.CompilerParams(vmem_limit_bytes=40 * 1024 * 1024),
        cost_estimate=BRIEF,
        name="attn_bwd",
    )(qkv, qkv, qkv, p, do, o)


FCUT = 768


def gelu_both(u):
    c = 0.7978845608028654
    square = u * u
    t = jnp.tanh(c * u * (1.0 + 0.044715 * square))
    half = 0.5 * (1.0 + t)
    slope = half + 0.5 * c * u * (1.0 - t * t) * (1.0 + 3 * 0.044715 * square)
    return u * half, slope


def ffn_fwd_kernel(rows_ref, win_ref, wout_ref, made_ref, sum_ref):
    step = pl.program_id(0)
    act = gelu_both(dot(rows_ref[...], win_ref[...]))[0].astype(BF16)
    part = dot(act, wout_ref[...])

    @pl.when(step == 0)
    def _():
        sum_ref[...] = part

    @pl.when(step > 0)
    def _():
        sum_ref[...] += part

    @pl.when(step == pl.num_programs(0) - 1)
    def _():
        made_ref[...] = sum_ref[...].astype(BF16)


def ffn_fwd(rows, w_in, w_out, level):
    count, width = rows.shape
    ff = w_in.shape[-1]
    whole = pl.BlockSpec((count, width), lambda i: (0, 0))
    return pl.pallas_call(
        ffn_fwd_kernel,
        grid=(ff // FCUT,),
        in_specs=[
            whole,
            pl.BlockSpec((None, None, width, FCUT), lambda i: (level, 0, 0, i)),
            pl.BlockSpec((None, None, FCUT, width), lambda i: (level, 0, i, 0)),
        ],
        out_specs=whole,
        out_shape=jax.ShapeDtypeStruct((count, width), BF16),
        scratch_shapes=[pltpu.VMEM((count, width), F32)],
        compiler_params=pltpu.CompilerParams(vmem_limit_bytes=40 * 1024 * 1024),
        cost_estimate=BRIEF,
        name="ffn_fwd",
    )(rows, w_in, w_out)


def ffn_both_kernel(
    rows_ref, dy_ref, miss_ref, router_ref, win_ref, wout_ref,
    made_ref, msg_ref, gin_ref, gout_ref, sum_ref, dsum_ref,
):
    step = pl.program_id(0)
    rows = rows_ref[...]
    dy = dy_ref[...]
    act, slope = gelu_both(dot(rows, win_ref[...]))
    act = act.astype(BF16)
    part = dot(act, wout_ref[...])
    dhid = (dot(dy, wout_ref[...], ((1,), (1,))) * slope).astype(BF16)
    dpart = dot(dhid, win_ref[...], ((1,), (1,)))
    gin_ref[...] = dot(rows, dhid, ((0,), (0,))).astype(BF16)
    gout = dot(act, dy, ((0,), (0,))).astype(BF16)
    per = gout_ref.shape[2]
    for j in range(gout.shape[0] // per):
        gout_ref[j % NZ, j // NZ] = gout[j * per : (j + 1) * per]

    @pl.when(step == 0)
    def _():
        sum_ref[...] = part
        dsum_ref[...] = dpart

    @pl.when(step > 0)
    def _():
        sum_ref[...] += part
        dsum_ref[...] += dpart

    @pl.when(step == pl.num_programs(0) - 1)
    def _():
        count = rows_ref.shape[0]
        made = sum_ref[...].astype(BF16)
        made_ref[...] = made
        product = dy.astype(F32) * made.astype(F32)
        gate = jnp.sum(product, -1, keepdims=True)
        dlogits = (gate * miss_ref[...]).astype(BF16)
        msg_ref[:count, :] = (dsum_ref[...] + dot(dlogits, router_ref[...])).astype(BF16)
        ones = jnp.ones((16, product.shape[1]), F32)
        msg_ref[count:, :] = jnp.zeros((16, product.shape[1]), BF16)
        msg_ref[count:, :count] = dot(ones, product, ((1,), (1,))).astype(BF16)


def ffn_both(rows, dy, miss, router_t, w_in, w_out, level):
    count, width = rows.shape
    ff = w_in.shape[-1]
    per = ff // (NX * NY * NZ)
    whole = pl.BlockSpec((count, width), lambda i: (0, 0))
    return pl.pallas_call(
        ffn_both_kernel,
        grid=(ff // FCUT,),
        in_specs=[
            whole,
            whole,
            pl.BlockSpec(miss.shape, lambda i: (0, 0)),
            pl.BlockSpec(router_t.shape, lambda i: (0, 0)),
            pl.BlockSpec((None, None, width, FCUT), lambda i: (level, 0, 0, i)),
            pl.BlockSpec((None, None, FCUT, width), lambda i: (level, 0, i, 0)),
        ],
        out_specs=[
            whole,
            pl.BlockSpec((count + 16, width), lambda i: (0, 0)),
            pl.BlockSpec((width, FCUT), lambda i: (0, i)),
            pl.BlockSpec((NZ, FCUT // per // NZ, per, width), lambda i: (0, i, 0, 0)),
        ],
        out_shape=[
            jax.ShapeDtypeStruct((count, width), BF16),
            jax.ShapeDtypeStruct((count + 16, width), BF16),
            jax.ShapeDtypeStruct((width, ff), BF16),
            jax.ShapeDtypeStruct((NZ, NX * NY, per, width), BF16),
        ],
        scratch_shapes=[pltpu.VMEM((count, width), F32), pltpu.VMEM((count, width), F32)],
        compiler_params=pltpu.CompilerParams(vmem_limit_bytes=48 * 1024 * 1024),
        cost_estimate=BRIEF,
        name="ffn_both",
    )(rows, dy, miss, router_t, w_in, w_out)


def norm_back_block(vector, gain, upstream):
    inverse = lax.rsqrt(jnp.mean(vector * vector, -1, keepdims=True) + EPS)
    scaled = upstream * gain
    grad_gain = jnp.sum(upstream * vector * inverse, 0, keepdims=True)
    grad_in = inverse * scaled - vector * (inverse * inverse * inverse) * jnp.mean(
        scaled * vector, -1, keepdims=True
    )
    return grad_in, grad_gain


def add_up(ref, value):
    @pl.when(pl.program_id(0) == 0)
    def _():
        ref[...] = value

    @pl.when(pl.program_id(0) > 0)
    def _():
        ref[...] += value


def middle_bwd_kernel(
    place_ref, m0_ref, m1_ref, m2_ref, m3_ref, middle_ref, up_ref, gain_ref, proj_ref,
    grad_ref, branch_ref, mixed_ref, gain_grad_ref,
):
    count = place_ref.shape[0]
    rows = jnp.concatenate([m0_ref[...], m1_ref[...], m2_ref[...], m3_ref[...]], 0)
    hot = place_ref[...] == lax.broadcasted_iota(jnp.int32, (count, rows.shape[0]), 1)
    normed_grad = dot(hot.astype(F32).astype(BF16), rows)
    grad, gain_grad = norm_back_block(middle_ref[...], gain_ref[...], normed_grad)
    grad = up_ref[...].astype(F32) + grad
    grad_ref[...] = grad
    branch = grad.astype(BF16)
    branch_ref[...] = branch
    mixed_ref[...] = dot(branch, proj_ref[...], ((1,), (1,))).astype(BF16)
    add_up(gain_grad_ref, gain_grad)


def middle_bwd(place, parts, middle, up, gain, proj):
    tok, width = middle.shape
    half = proj.shape[0]
    cap = BLK // 2
    whole = lambda i: (0, 0)
    block = lambda i: (i, 0)
    return pl.pallas_call(
        middle_bwd_kernel,
        grid=(tok // BLK,),
        in_specs=[pl.BlockSpec((BLK, 1), block)]
        + [pl.BlockSpec((cap, width), block)] * 4
        + [
            pl.BlockSpec((BLK, width), block),
            pl.BlockSpec((BLK, width), block),
            pl.BlockSpec((1, width), whole),
            pl.BlockSpec((half, width), whole),
        ],
        out_specs=[
            pl.BlockSpec((BLK, width), block),
            pl.BlockSpec((BLK, width), block),
            pl.BlockSpec((BLK, half), block),
            pl.BlockSpec((1, width), whole),
        ],
        out_shape=[
            jax.ShapeDtypeStruct((tok, width), F32),
            jax.ShapeDtypeStruct((tok, width), BF16),
            jax.ShapeDtypeStruct((tok, half), BF16),
            jax.ShapeDtypeStruct((1, width), F32),
        ],
        compiler_params=pltpu.CompilerParams(vmem_limit_bytes=32 * 1024 * 1024),
        cost_estimate=BRIEF,
        name="middle_bwd",
    )(place, *parts, middle, up, gain[None], proj)


def first_bwd_kernel(
    place_ref, own_ref, near_ref, stream_ref, grad_ref, gain_ref, gate_ref,
    up_ref, made_ref, gain_grad_ref,
):
    count = place_ref.shape[0]
    first_grad = own_ref[...].astype(F32) + near_ref[...].astype(F32)
    grad, gain_grad = norm_back_block(stream_ref[...], gain_ref[...], first_grad)
    grad = grad_ref[...] + grad
    up_ref[...] = grad
    hot = place_ref[...] == lax.broadcasted_iota(jnp.int32, (count, BLK), 1)
    gated = (gate_ref[...] * grad).astype(BF16)
    made = dot(hot.astype(F32).astype(BF16), gated, ((0,), (0,)))
    made_ref[...] = made[: made_ref.shape[0]].astype(BF16)
    add_up(gain_grad_ref, gain_grad)


def first_bwd(place, own, near, stream, grad, gain, gate):
    tok, width = stream.shape
    cap = BLK // 2
    whole = lambda i: (0, 0)
    block = lambda i: (i, 0)
    wide = pl.BlockSpec((BLK, width), block)
    return pl.pallas_call(
        first_bwd_kernel,
        grid=(tok // BLK,),
        in_specs=[
            pl.BlockSpec((BLK, 1), block), wide, wide, wide, wide,
            pl.BlockSpec((1, width), whole), pl.BlockSpec((BLK, 1), block),
        ],
        out_specs=[wide, pl.BlockSpec((cap, width), block), pl.BlockSpec((1, width), whole)],
        out_shape=[
            jax.ShapeDtypeStruct((tok, width), F32),
            jax.ShapeDtypeStruct((tok // 2, width), BF16),
            jax.ShapeDtypeStruct((1, width), F32),
        ],
        compiler_params=pltpu.CompilerParams(vmem_limit_bytes=32 * 1024 * 1024),
        cost_estimate=BRIEF,
        name="first_bwd",
    )(place, own, near, stream, grad, gain[None], gate)


def pack_kernel(normed_ref, qkv_ref, mixed_ref, branch_ref, small_ref, out_ref):
    wide = qkv_ref.shape[1]
    rows = mixed_ref.shape[1]
    half = branch_ref.shape[1] // 2
    out_ref[:, :wide] = dot(normed_ref[...], qkv_ref[...], ((0,), (0,))).astype(BF16)
    proj = dot(mixed_ref[...], branch_ref[...], ((0,), (0,))).astype(BF16)
    out_ref[:rows, wide : wide + half] = proj[:, :half]
    out_ref[rows:, wide : wide + half] = proj[:, half:]
    out_ref[:, wide + half :] = small_ref[...]


def pack_table(normed, qkv_grad, mixed, branch_grad, small):
    columns = qkv_grad.shape[1] + branch_grad.shape[1] // 2 + small.shape[1]
    return pl.pallas_call(
        pack_kernel,
        out_shape=jax.ShapeDtypeStruct((normed.shape[1], columns), BF16),
        compiler_params=pltpu.CompilerParams(vmem_limit_bytes=40 * 1024 * 1024),
        cost_estimate=BRIEF,
        name="pack_table",
    )(normed, qkv_grad, mixed, branch_grad, small)


def rep_index(x, yh, z):
    return ((x % NX) * NY + yh % NY) * NZ + z % NZ


def rep_shift(dx, dy, dz):
    return [
        (rep_index(x, y, z), rep_index(x + dx, y + dy, z + dz))
        for x in range(NX)
        for y in range(NY)
        for z in range(NZ)
    ]


def y_shift(dy, flip):
    reps = NX * NY * NZ
    pairs = []
    for x in range(NX):
        for yh in range(NY):
            for z in range(NZ):
                for yl in range(2):
                    for core in range(2):
                        y = (yh * 2 + yl + dy) % 4
                        source = (yl * 2 + core) * reps + rep_index(x, yh, z)
                        target = ((y % 2) * 2 + (core ^ flip)) * reps + rep_index(x, y // 2, z)
                        pairs.append((source, target))
    return pairs


def swap(value, bits):
    return lax.ppermute(value, "shard", [(s, s ^ bits) for s in range(4)])


def along_y(value, dy, flip):
    return lax.ppermute(value, ("shard", "rep"), y_shift(dy, flip))


def spread(value):
    near = swap(value, 1)
    far = swap(value, 2)
    return (value, near, far, swap(far, 1))


def in_order(values, me):
    rows = values[0].shape[0]
    whole = jnp.zeros((4 * rows,) + values[0].shape[1:], values[0].dtype)
    for r, value in enumerate(values):
        whole = lax.dynamic_update_slice_in_dim(whole, value, (me ^ r) * rows, 0)
    return whole


def take(array, index, axis=0):
    return lax.dynamic_index_in_dim(array, index, axis, keepdims=False)


def after(values, on):
    return lax.optimization_barrier((values, on))[0]


def exchange(array, axis, here, size, shift):
    got = [take(array, here, axis)]
    for step in range(1, size):
        got.append(lax.ppermute(take(array, (here + step) % size, axis), "rep", shift(step)))
    return got


def total(parts):
    return sum(part.astype(F32) for part in parts)


def x_parts(array, axis, place):
    return exchange(array, axis, place[0], NX, lambda s: rep_shift(s, 0, 0))


def y_parts(array, axis, place):
    return exchange(array, axis, place[1], NY, lambda s: rep_shift(0, s, 0))


def z_parts(array, axis, place):
    return exchange(array, axis, place[2], NZ, lambda s: rep_shift(0, 0, s))


def x_groups():
    return [[rep_index(x, y, z) for x in range(NX)] for y in range(NY) for z in range(NZ)]


def z_groups():
    return [[rep_index(x, y, z) for z in range(NZ)] for x in range(NX) for y in range(NY)]


def inner_first(inner):
    return lax.psum_scatter(
        inner, "rep", scatter_dimension=0, tiled=True, axis_index_groups=x_groups()
    )


def inner_y(part, place):
    return y_parts(part.reshape(NY, part.shape[0] // NY, part.shape[1]), 0, place)


def outer_first(outer):
    return lax.all_to_all(
        outer, "rep", split_axis=0, concat_axis=0, tiled=True, axis_index_groups=z_groups()
    )


def outer_sum(parts):
    return jnp.sum(parts.astype(F32), 0).astype(BF16)


def outer_y(parts, place):
    part = outer_sum(parts)
    return y_parts(part.reshape((NX, NY) + part.shape[1:]), 1, place)


def on_device(
    tokens,
    lengths,
    routes,
    attn_in,
    attn_proj,
    norm_first,
    norm_second,
    rel_bias,
    router,
    expert_in,
    expert_out,
    cotangent,
):
    me = lax.axis_index("shard")
    rep = lax.axis_index("rep")
    place = (rep // (NY * NZ), (rep // NZ) % NY, rep % NZ)
    core = me & 1
    odd = core == 1
    levels, own_rows, width3 = attn_in.shape
    width = width3 // 3
    half = width // 2
    tok = 4 * BLK
    heads = rel_bias.shape[2]
    heads_own = heads // 2
    buckets = rel_bias.shape[1]
    experts = router.shape[2]
    cap = BLK // 2

    def column_halves(block):
        parts = [block[..., i * half : (i + 1) * half] for i in range(6)]
        low = jnp.concatenate(parts[0::2], -1)
        high = jnp.concatenate(parts[1::2], -1)
        return jnp.where(odd, high, low), jnp.where(odd, low, high)

    cut = own_rows // 2
    route_row = jnp.zeros((16, width), BF16).at[0, :BLK].set(routes[0].astype(BF16))

    def fetch(own, axis):
        low = lax.slice_in_dim(own, 0, cut, axis=axis)
        high = lax.slice_in_dim(own, cut, 2 * cut, axis=axis)
        return along_y(low, 1, 0), along_y(high, -1, 0)

    def build_qkv(own, far):
        mine, others = column_halves(own)
        far_mine, far_others = column_halves(jnp.concatenate(far, 0))
        return in_order((mine, swap(others, 1), far_mine, swap(far_others, 1)), me)

    def build_proj(own, far):
        far = jnp.concatenate(far, 1)
        near = swap(jnp.stack([own, far], 0), 1)
        return [
            in_order((own[level], near[0, level], far[level], near[1, level]), me)
            for level in range(levels)
        ]

    w_qkv0 = build_qkv(attn_in[0], fetch(attn_in[0], 0))
    token_parts = spread(jnp.concatenate([tokens[0], route_row], 0))
    x0 = in_order([part[:BLK] for part in token_parts], me)
    route_parts = [part[BLK, :BLK].astype(jnp.int32) for part in token_parts]
    far_proj = fetch(after(attn_proj, w_qkv0), 1)

    position = jnp.arange(tok, dtype=jnp.int32)
    ends = jnp.cumsum(lengths[0])
    doc = jnp.sum((position[:, None] >= ends[None, :]).astype(jnp.int32), -1).astype(F32)
    docq, dock = doc[:, None], doc[None, :]
    own_bias = jnp.where(odd, rel_bias[:, :, heads_own:], rel_bias[:, :, :heads_own])
    turn = jnp.arange(2 * BLK, dtype=jnp.int32)
    line_offset = (
        BLK * (jnp.arange(8, dtype=jnp.int32) - 2)[:, None]
        + jnp.where(turn < BLK, turn, turn - 2 * BLK)[None]
    )
    line_hot = (
        bucket_of(line_offset)[None] == jnp.arange(buckets, dtype=jnp.int32)[:, None, None]
    ).astype(F32)
    lines = jnp.einsum("lbh,bdm->lhdm", own_bias, line_hot, precision=HIGH)
    lines = lines.reshape(levels, heads_own // 2, 2, 8, 2 * BLK)
    route = in_order([part[None] for part in route_parts], me)
    onehot = (route[..., None] == jnp.arange(experts, dtype=jnp.int32)).astype(jnp.int32)
    slot = jnp.sum(jnp.cumsum(onehot, axis=1) * onehot, -1) - 1
    dispatch = (
        (route == me)[:, None, :] & (slot[:, None, :] == jnp.arange(cap)[None, :, None])
    ).astype(BF16)
    at_slot = jnp.arange(4, dtype=jnp.int32)[:, None] * cap + slot
    collect = [
        (
            (route.reshape(tok) == (me ^ r))[:, None]
            & (at_slot.reshape(tok)[:, None] == jnp.arange(4 * cap)[None, :])
        ).astype(BF16)
        for r in range(4)
    ]
    chosen = onehot.reshape(tok, experts).astype(F32)
    spot = ((route ^ me) * cap + slot).reshape(tok, 1)

    router_ts = [
        jnp.pad(router[level].T, ((0, BLK - experts), (0, 0))) for level in range(levels)
    ]
    router_ts, spot, collect, chosen, x0 = lax.optimization_barrier(
        (router_ts, spot, collect, chosen, x0)
    )

    def rows_of(stream):
        return jnp.einsum(
            "bct,btd->bcd", dispatch, stream.reshape(4, BLK, -1), preferred_element_type=F32
        ).reshape(4 * cap, -1)

    def gathered(parts):
        return (
            dot(collect[0], parts[0])
            + dot(collect[1], parts[1])
            + dot(collect[2], parts[2])
            + dot(collect[3], parts[3])
        )

    def cols_of(array):
        return lax.dynamic_slice_in_dim(array, me * own_rows, own_rows, 1)

    saved = []
    misses = []
    w_qkv = [w_qkv0]
    stream = x0.astype(F32)
    for level in range(levels):
        normed = rms_norm(stream, norm_first[level]).astype(BF16)
        qkv = dot(normed, w_qkv[level]).astype(BF16)
        if level > 0:
            qkv, cot_own = lax.optimization_barrier((qkv, cotangent[0]))
            cot = in_order(spread(cot_own), me)
        o_own, probs = attn_fwd(qkv, lines[level], docq, dock)
        if level == 0:
            w_proj = build_proj(*after((attn_proj, far_proj), o_own))
            next_in = after(attn_in[1], o_own)
            next_far = fetch(next_in, 0)
        o_near = swap(o_own, 1)
        mixed = jnp.concatenate(
            [jnp.where(odd, o_near, o_own), jnp.where(odd, o_own, o_near)], 1
        )
        middle = stream + dot(mixed, w_proj[level])
        normed_two = rms_norm(middle, norm_second[level]).astype(BF16)
        logits = dot(normed_two, router[level])
        route_probs = jax.nn.softmax(logits, -1)
        gate = jnp.sum(route_probs * chosen, -1)
        rows = rows_of(normed_two).astype(BF16)
        slot_probs = jnp.einsum(
            "bct,bte->bce", dispatch, route_probs.reshape(4, BLK, experts).astype(BF16),
            preferred_element_type=F32,
        ).reshape(4 * cap, experts)
        miss = jnp.pad(
            (jnp.arange(experts) == me).astype(F32)[None] - slot_probs,
            ((0, 0), (0, BLK - experts)),
        )
        misses.append(miss)
        saved.append(
            (stream, normed, qkv, o_own, probs, mixed, middle, normed_two, route_probs, gate, rows)
        )
        if level < levels - 1:
            made = ffn_fwd(rows, expert_in, expert_out, level)
            w_qkv.append(build_qkv(*after((next_in, next_far), made)))
            made_parts = spread(made)
            w_proj_owns = [lax.dynamic_slice_in_dim(w, core * half, half, 0) for w in w_proj]
            middle, gate, misses, w_proj_owns, far_made = lax.optimization_barrier(
                (middle, gate, misses, w_proj_owns, made_parts[2])
            )
            made_parts = made_parts[:2] + (far_made,) + made_parts[3:]
            stream = middle + gate[:, None] * gathered(made_parts)

    def go_home(made, middle, gate):
        blocks = made.reshape(4, cap, width)
        home = [take(blocks, me)] + [swap(take(blocks, me ^ r), r) for r in (1, 2, 3)]
        own_route, own_slot = take(route, me), take(slot, me)
        back = sum(
            dot(
                (
                    (own_route == (me ^ r))[:, None]
                    & (own_slot[:, None] == jnp.arange(cap)[None, :])
                ).astype(BF16),
                home[r],
            )
            for r in range(4)
        )
        own_gate = lax.dynamic_slice_in_dim(gate, me * BLK, BLK, 0)
        own_after = lax.dynamic_slice_in_dim(middle, me * BLK, BLK, 0)
        result = (own_after + own_gate[:, None] * back).astype(BF16)[None]
        return result

    def pack(normed, mixed, normed_two, branch_grad, qkv_grad, bias_sums, message_parts,
             route_probs, grad_first, grad_second):
        chip_rows = lambda array, axis: lax.dynamic_slice_in_dim(
            array, (me >> 1) * 2 * own_rows, 2 * own_rows, axis
        )
        token_gate_grad = sum(
            dot(collect[r], message_parts[r][4 * cap :, : 4 * cap], ((1,), (1,))) for r in range(4)
        )[:, :1]
        logit_grad = token_gate_grad * (chosen - route_probs)
        own_vec = lambda vec: lax.dynamic_slice_in_dim(vec, me * own_rows, own_rows, 0)[:, None]
        grad_router = dot(cols_of(normed_two), logit_grad.astype(BF16), ((0,), (0,)))
        own = jnp.concatenate([own_vec(grad_first), own_vec(grad_second), grad_router], 1)
        own = jnp.where(
            (jnp.arange(2) == core)[:, None, None], own[None], jnp.zeros_like(own)[None]
        )
        count = after(jnp.arange(BLK, dtype=jnp.int32), branch_grad)
        offset = (
            BLK * (jnp.arange(5, dtype=jnp.int32) - 2)[:, None, None]
            + count[None, None, :]
            - count[None, :, None]
        )
        bucket_id = bucket_of(offset)
        bucket_hot = bucket_id[None] == jnp.arange(buckets, dtype=jnp.int32)[:, None, None, None]
        bias_own = jnp.einsum(
            "hdij,bdij->bh", bias_sums, bucket_hot.astype(BF16), preferred_element_type=F32
        )
        none = jnp.zeros_like(bias_own)
        bias_all = jnp.where(
            odd,
            jnp.concatenate([none, bias_own], 1),
            jnp.concatenate([bias_own, none], 1),
        ).reshape(-1)
        bias_rows = lax.dynamic_slice_in_dim(
            bias_all, (me >> 1) * bias_all.shape[0] // 2, bias_all.shape[0] // 2, 0
        ).reshape(2, 32, -1)
        per = own_rows // 32
        bias_rows = jnp.pad(bias_rows, ((0, 0), (0, 0), (0, per - bias_rows.shape[2])))
        small = jnp.concatenate([own, bias_rows.reshape(2, own_rows, 1)], 2)
        small = jnp.pad(small, ((0, 0), (0, 0), (0, BLK - small.shape[2]))).astype(BF16)
        table = pack_table(
            chip_rows(normed, 1), qkv_grad, cols_of(mixed), branch_grad, small.reshape(2 * own_rows, -1)
        )
        table = table.reshape(2, NX, NY, NZ * per, table.shape[1])
        return y_parts(table, 2, place)

    upstream = cot
    packs = [None] * levels
    inner_parts = [None] * levels
    outer_parts = [None] * levels
    for level in reversed(range(levels)):
        (stream, normed, qkv, o_own, probs, mixed, middle, normed_two, route_probs, gate,
         rows) = saved[level]
        if level == levels - 1:
            made_grad = rows_of((gate[:, None] * upstream.astype(F32)).astype(BF16)).astype(BF16)
        w_proj_own = w_proj_owns[level]
        made_grad, upstream, w_proj_own, spot = lax.optimization_barrier(
            (made_grad, upstream, w_proj_own, spot)
        )
        made, message, inner, outer = ffn_both(
            rows, made_grad, misses[level], router_ts[level], expert_in, expert_out, level
        )
        message_parts = spread(message)
        far_part = message_parts[2]
        if level == levels - 1:
            last = (made, middle, gate)
        waited = (far_part,)
        if level < levels - 1:
            over = level + 1
            waited = (far_part, outer_parts[over], inner_parts[over])
        inner, outer, upstream, middle, route_probs, waited = lax.optimization_barrier(
            (inner, outer, upstream, middle, route_probs, waited)
        )
        inner_parts[level] = inner_first(inner)
        outer_parts[level] = outer_first(outer)
        if level < levels - 1:
            outer_parts[over] = outer_y(waited[1], place)
            inner_parts[over] = inner_y(waited[2], place)

        after_grad, branch_grad, mixed_grad, grad_second = middle_bwd(
            spot, message_parts, middle, upstream, norm_second[level], w_proj_own
        )
        grad_second = grad_second[0]
        qkv_grad, bias_sums = attn_bwd(qkv, probs, mixed_grad, o_own)
        if level < levels - 1:
            pending, stream = after((pending, stream), qkv_grad)
            packs[level + 1] = pack(*pending)
        first_part = dot(qkv_grad, w_qkv[level], ((1,), (1,))).astype(BF16)
        near_first = swap(first_part, 1)
        if level > 0:
            upstream, made_grad, grad_first = first_bwd(
                spot, first_part, near_first, stream, after_grad, norm_first[level],
                saved[level - 1][9][:, None],
            )
            grad_first = grad_first[0]
        else:
            input_side, grad_first = norm_back(
                stream, norm_first[level], first_part.astype(F32) + near_first.astype(F32)
            )
            upstream = after_grad + input_side
        pending = (normed, mixed, normed_two, branch_grad, qkv_grad, bias_sums, message_parts,
                   route_probs, grad_first, grad_second)
        if level < levels - 1:
            packs[level] = pack(*pending)

    own_parts = [part[0] for part in packs]

    outer_low, inner_low = after((outer_parts[0], inner_parts[0]), own_parts)
    outer_low = outer_sum(outer_low)
    last, inner_top, outer_top = after((last, inner_parts[1], outer_parts[1]), outer_low)
    inner_top = total(inner_top).astype(BF16)
    outer_top = total(outer_top).astype(BF16)
    rows_in = inner_low.shape[0] // (NY * NZ)
    inner_all = jnp.concatenate(
        [
            inner_low.reshape(NY, NZ, rows_in, -1),
            inner_top.reshape(1, NZ, rows_in, -1),
        ],
        0,
    )
    outer_all = jnp.concatenate(
        [outer_low.reshape((NX, NY) + outer_low.shape[1:]), outer_top[:, None]], 1
    )
    inner_all = z_parts(inner_all, 1, place)
    outer_all = x_parts(outer_all, 0, place)
    inner_all, outer_all, packs, last = lax.optimization_barrier(
        (inner_all, outer_all, packs, last)
    )
    result = go_home(*last)
    inner_all = total(inner_all)
    outer_all = total(outer_all)
    inner_low = total(y_parts(inner_all[:NY].astype(BF16), 0, place))
    outer_low = total(y_parts(outer_all[:NY].astype(BF16), 0, place))
    expert_in_grad = jnp.stack([inner_low, inner_all[NY]], 0)[:, None]
    expert_out_grad = jnp.stack([outer_low, outer_all[NY]], 0)[:, None]
    table = jnp.stack([total(part).astype(BF16) for part in packs], 0)
    table = total(x_parts(table, 2, place)).astype(BF16)
    per = own_rows // 32
    table = total(z_parts(table.reshape(levels, 2, NZ, per, -1), 2, place))
    mine = take(table, core, 1)
    near = swap(take(table, core ^ 1, 1), 1)
    pieces = []
    for part in range(3):
        a = mine[..., part * half : (part + 1) * half]
        b = near[..., part * half : (part + 1) * half]
        pieces += [jnp.where(odd, b, a), jnp.where(odd, a, b)]
    attn_in_grad = jnp.concatenate(pieces, -1)
    at = width3 // 2
    attn_proj_grad = jnp.concatenate(
        [table[:, 0, :, at : at + half], table[:, 1, :, at : at + half]], -1
    )
    at += half
    few = buckets * heads // 128
    stacked = (
        attn_in_grad,
        attn_proj_grad,
        mine[:, :, at],
        mine[:, :, at + 1],
        mine[:, :few, at + 2 + experts] + near[:, :few, at + 2 + experts],
        mine[:, :, at + 2 : at + 2 + experts],
    )

    own_up = lax.dynamic_slice_in_dim(upstream, me * BLK, BLK, 0)
    tokens_grad = own_up.astype(BF16)[None]
    return (result, tokens_grad, *stacked, expert_in_grad, expert_out_grad)


def solution(mesh):
    return jax.shard_map(
        on_device,
        mesh=mesh,
        in_specs=(
            P("rep", "shard", None),
            P("rep", None),
            P("rep", "shard"),
            P(None, "shard", None),
            P(None, "shard", None),
            P(),
            P(),
            P(),
            P(),
            P(None, "shard", None, None),
            P(None, "shard", None, None),
            P("rep", "shard", None),
        ),
        out_specs=(
            P("rep", "shard", None),
            P("rep", "shard", None),
            P(None, ("shard", "rep"), None),
            P(None, ("shard", "rep"), None),
            P(None, ("shard", "rep")),
            P(None, ("shard", "rep")),
            P(None, ("shard", "rep")),
            P(None, ("shard", "rep"), None),
            P(None, "shard", "rep", None),
            P(None, "shard", "rep", None),
        ),
        check_vma=False,
    )
```

```python
import functools

import jax
import jax.numpy as jnp
from jax import lax
from jax.experimental import pallas as pl
from jax.experimental.pallas import tpu as pltpu
from jax.sharding import PartitionSpec as P

EPS = 1e-06
SCALE = 0.125
NEG = -1e30
THRESHOLDS = (12, 16, 23, 32, 46, 64, 91)
HIGH = lax.Precision.HIGHEST
F32 = jnp.float32
BF16 = jnp.bfloat16
BRIEF = pl.CostEstimate(flops=10**6, bytes_accessed=10**5, transcendentals=0)
BLK = 128
NX, NY, NZ = 4, 2, 4


def bucket_of(offset):
    distance = jnp.abs(offset)
    far_bucket = 8 + sum(((distance >= threshold).astype(jnp.int32) for threshold in THRESHOLDS))
    bucket_id = jnp.where(distance < 8, distance, far_bucket)
    return bucket_id + 16 * (offset > 0).astype(jnp.int32)


def rms_norm(vector, gain_vec):
    inverse = lax.rsqrt(jnp.mean(vector * vector, -1, keepdims=True) + EPS)
    return vector * inverse * gain_vec


def norm_back(vector, gain_vec, upstream):
    inverse = lax.rsqrt(jnp.mean(vector * vector, -1, keepdims=True) + EPS)
    scaled = upstream * gain_vec
    grad_gain = jnp.sum(upstream * vector * inverse, 0)
    grad_in = inverse * scaled - vector * (inverse * inverse * inverse) * jnp.mean(
        scaled * vector, -1, keepdims=True
    )
    return (grad_in, grad_gain)


def gelu_tanh(vector):
    return jax.nn.gelu(vector, approximate=True)


def dot(a, b, dims=((1,), (0,))):
    return lax.dot_general(a, b, (dims, ((), ())), preferred_element_type=F32)


def attn_fwd_kernel(q_ref, k_ref, v_ref, line_ref, docq_ref, dock_ref, o_ref, p_ref):
    tok = q_ref.shape[0]
    nblk = tok // BLK
    first = lax.broadcasted_iota(jnp.int32, (1, BLK), 1) < BLK // 2
    k = k_ref[...]
    v = v_ref[...]
    bias = []
    for hh in range(2):
        blocks = []
        for d in range(5):
            line = jnp.broadcast_to(line_ref[0, hh, d : d + 1, :], (BLK, 2 * BLK))
            if d in (1, 2, 3):
                line = pltpu.roll(line, 0, 1, stride=1, stride_axis=0)
            blocks.append(line[:, :BLK])
        bias.append(blocks)
    for i in range(nblk):
        rows = slice(i * BLK, (i + 1) * BLK)
        same = docq_ref[rows, :] == dock_ref[...]
        q = q_ref[rows, :]
        outs = []
        for hh in range(2):
            mine = first if hh == 0 else jnp.logical_not(first)
            qm = jnp.where(mine, q, jnp.zeros_like(q))
            s = dot(qm, k, ((1,), (1,))) * SCALE
            spread_bias = jnp.concatenate(
                [bias[hh][max(-2, min(2, j - i)) + 2] for j in range(nblk)], axis=1
            )
            s = jnp.where(same, s + spread_bias, NEG)
            e = jnp.exp(s - jnp.max(s, -1, keepdims=True))
            p = (e * (1.0 / jnp.sum(e, -1, keepdims=True))).astype(BF16)
            p_ref[hh, rows, :] = p
            outs.append(dot(p, v))
        o_ref[rows, :] = jnp.where(first, outs[0], outs[1]).astype(BF16)


def attn_fwd(qkv, lines, docq, dock):
    tok, width = qkv.shape
    heads_w = width // 3
    pairs = heads_w // BLK
    return pl.pallas_call(
        attn_fwd_kernel,
        grid=(pairs,),
        in_specs=[
            pl.BlockSpec((tok, BLK), lambda h: (0, h)),
            pl.BlockSpec((tok, BLK), lambda h: (0, pairs + h)),
            pl.BlockSpec((tok, BLK), lambda h: (0, 2 * pairs + h)),
            pl.BlockSpec((1, 2, 8, 2 * BLK), lambda h: (h, 0, 0, 0)),
            pl.BlockSpec((tok, 1), lambda h: (0, 0)),
            pl.BlockSpec((1, tok), lambda h: (0, 0)),
        ],
        out_specs=[
            pl.BlockSpec((tok, BLK), lambda h: (0, h)),
            pl.BlockSpec((2, tok, tok), lambda h: (h, 0, 0)),
        ],
        out_shape=[
            jax.ShapeDtypeStruct((tok, heads_w), BF16),
            jax.ShapeDtypeStruct((2 * pairs, tok, tok), BF16),
        ],
        compiler_params=pltpu.CompilerParams(vmem_limit_bytes=40 * 1024 * 1024),
        cost_estimate=BRIEF,
        name="attn_fwd",
    )(qkv, qkv, qkv, lines, docq, dock)


def attn_bwd_kernel(q_ref, k_ref, v_ref, p_ref, do_ref, o_ref, dqkv_ref, m_ref, ds_ref):
    tok = q_ref.shape[0]
    nblk = tok // BLK
    pairs = pl.num_programs(0)
    step = pl.program_id(0)
    first = lax.broadcasted_iota(jnp.int32, (1, BLK), 1) < BLK // 2
    k = k_ref[...]
    v = v_ref[...]
    q = q_ref[...]
    do = do_ref[...]
    dk = jnp.zeros((tok, BLK), F32)
    dv = jnp.zeros((tok, BLK), F32)
    dqs = []
    for hh in range(2):
        mine = first if hh == 0 else jnp.logical_not(first)
        dom = jnp.where(mine, do, jnp.zeros_like(do))
        qm = jnp.where(mine, q, jnp.zeros_like(q))
        parts = [None] * 5
        dq_rows = []
        for i in range(nblk):
            rows = slice(i * BLK, (i + 1) * BLK)
            doi = dom[rows, :]
            dp = dot(doi, v, ((1,), (1,)))
            base = jnp.sum(
                doi.astype(F32) * o_ref[rows, :].astype(F32), -1, keepdims=True
            )
            ds = p_ref[hh, rows, :].astype(F32) * (dp - base)
            for j in range(nblk):
                d = max(-2, min(2, j - i)) + 2
                piece = ds[:, j * BLK : (j + 1) * BLK]
                parts[d] = piece if parts[d] is None else parts[d] + piece
            dsb = ds.astype(BF16)
            ds_ref[rows, :] = dsb
            dq_rows.append(dot(dsb, k))
        for d in range(5):
            m_ref[hh, d] = parts[d].astype(BF16)
        dqs.append(dq_rows)
        dk = dk + dot(ds_ref[...], qm, ((0,), (0,)))
        dv = dv + dot(p_ref[hh], dom, ((0,), (0,)))
    at = lambda part: pl.ds(pl.multiple_of((part * pairs + step) * BLK, BLK), BLK)
    for i in range(nblk):
        rows = slice(i * BLK, (i + 1) * BLK)
        dqkv_ref[rows, at(0)] = (jnp.where(first, dqs[0][i], dqs[1][i]) * SCALE).astype(BF16)
    dqkv_ref[:, at(1)] = (dk * SCALE).astype(BF16)
    dqkv_ref[:, at(2)] = dv.astype(BF16)


def attn_bwd(qkv, p, do, o):
    tok, width = qkv.shape
    heads_w = width // 3
    pairs = heads_w // BLK
    return pl.pallas_call(
        attn_bwd_kernel,
        grid=(pairs,),
        in_specs=[
            pl.BlockSpec((tok, BLK), lambda h: (0, h)),
            pl.BlockSpec((tok, BLK), lambda h: (0, pairs + h)),
            pl.BlockSpec((tok, BLK), lambda h: (0, 2 * pairs + h)),
            pl.BlockSpec((2, tok, tok), lambda h: (h, 0, 0)),
            pl.BlockSpec((tok, BLK), lambda h: (0, h)),
            pl.BlockSpec((tok, BLK), lambda h: (0, h)),
        ],
        out_specs=[
            pl.BlockSpec((tok, width), lambda h: (0, 0)),
            pl.BlockSpec((2, 5, BLK, BLK), lambda h: (h, 0, 0, 0)),
        ],
        out_shape=[
            jax.ShapeDtypeStruct((tok, width), BF16),
            jax.ShapeDtypeStruct((2 * pairs, 5, BLK, BLK), BF16),
        ],
        scratch_shapes=[pltpu.VMEM((tok, tok), BF16)],
        compiler_params=pltpu.CompilerParams(vmem_limit_bytes=40 * 1024 * 1024),
        cost_estimate=BRIEF,
        name="attn_bwd",
    )(qkv, qkv, qkv, p, do, o)


FCUT = 768


def gelu_both(u):
    c = 0.7978845608028654
    square = u * u
    t = jnp.tanh(c * u * (1.0 + 0.044715 * square))
    half = 0.5 * (1.0 + t)
    slope = half + 0.5 * c * u * (1.0 - t * t) * (1.0 + 3 * 0.044715 * square)
    return u * half, slope


def ffn_fwd_kernel(rows_ref, win_ref, wout_ref, made_ref, sum_ref):
    step = pl.program_id(0)
    act = gelu_both(dot(rows_ref[...], win_ref[...]))[0].astype(BF16)
    part = dot(act, wout_ref[...])

    @pl.when(step == 0)
    def _():
        sum_ref[...] = part

    @pl.when(step > 0)
    def _():
        sum_ref[...] += part

    @pl.when(step == pl.num_programs(0) - 1)
    def _():
        made_ref[...] = sum_ref[...].astype(BF16)


def ffn_fwd(rows, w_in, w_out, level):
    count, width = rows.shape
    ff = w_in.shape[-1]
    whole = pl.BlockSpec((count, width), lambda i: (0, 0))
    return pl.pallas_call(
        ffn_fwd_kernel,
        grid=(ff // FCUT,),
        in_specs=[
            whole,
            pl.BlockSpec((None, None, width, FCUT), lambda i: (level, 0, 0, i)),
            pl.BlockSpec((None, None, FCUT, width), lambda i: (level, 0, i, 0)),
        ],
        out_specs=whole,
        out_shape=jax.ShapeDtypeStruct((count, width), BF16),
        scratch_shapes=[pltpu.VMEM((count, width), F32)],
        compiler_params=pltpu.CompilerParams(vmem_limit_bytes=40 * 1024 * 1024),
        cost_estimate=BRIEF,
        name="ffn_fwd",
    )(rows, w_in, w_out)


def ffn_both_kernel(
    rows_ref, dy_ref, miss_ref, router_ref, win_ref, wout_ref,
    made_ref, msg_ref, gin_ref, gout_ref, sum_ref, dsum_ref,
):
    step = pl.program_id(0)
    rows = rows_ref[...]
    dy = dy_ref[...]
    act, slope = gelu_both(dot(rows, win_ref[...]))
    act = act.astype(BF16)
    part = dot(act, wout_ref[...])
    dhid = (dot(dy, wout_ref[...], ((1,), (1,))) * slope).astype(BF16)
    dpart = dot(dhid, win_ref[...], ((1,), (1,)))
    gin_ref[...] = dot(rows, dhid, ((0,), (0,))).astype(BF16)
    gout = dot(act, dy, ((0,), (0,))).astype(BF16)
    per = gout_ref.shape[2]
    for j in range(gout.shape[0] // per):
        gout_ref[j % NZ, j // NZ] = gout[j * per : (j + 1) * per]

    @pl.when(step == 0)
    def _():
        sum_ref[...] = part
        dsum_ref[...] = dpart

    @pl.when(step > 0)
    def _():
        sum_ref[...] += part
        dsum_ref[...] += dpart

    @pl.when(step == pl.num_programs(0) - 1)
    def _():
        count = rows_ref.shape[0]
        made = sum_ref[...].astype(BF16)
        made_ref[...] = made
        product = dy.astype(F32) * made.astype(F32)
        gate = jnp.sum(product, -1, keepdims=True)
        dlogits = (gate * miss_ref[...]).astype(BF16)
        msg_ref[:count, :] = (dsum_ref[...] + dot(dlogits, router_ref[...])).astype(BF16)
        ones = jnp.ones((16, product.shape[1]), F32)
        msg_ref[count:, :] = jnp.zeros((16, product.shape[1]), BF16)
        msg_ref[count:, :count] = dot(ones, product, ((1,), (1,))).astype(BF16)


def ffn_both(rows, dy, miss, router_t, w_in, w_out, level):
    count, width = rows.shape
    ff = w_in.shape[-1]
    per = ff // (NX * NY * NZ)
    whole = pl.BlockSpec((count, width), lambda i: (0, 0))
    return pl.pallas_call(
        ffn_both_kernel,
        grid=(ff // FCUT,),
        in_specs=[
            whole,
            whole,
            pl.BlockSpec(miss.shape, lambda i: (0, 0)),
            pl.BlockSpec(router_t.shape, lambda i: (0, 0)),
            pl.BlockSpec((None, None, width, FCUT), lambda i: (level, 0, 0, i)),
            pl.BlockSpec((None, None, FCUT, width), lambda i: (level, 0, i, 0)),
        ],
        out_specs=[
            whole,
            pl.BlockSpec((count + 16, width), lambda i: (0, 0)),
            pl.BlockSpec((width, FCUT), lambda i: (0, i)),
            pl.BlockSpec((NZ, FCUT // per // NZ, per, width), lambda i: (0, i, 0, 0)),
        ],
        out_shape=[
            jax.ShapeDtypeStruct((count, width), BF16),
            jax.ShapeDtypeStruct((count + 16, width), BF16),
            jax.ShapeDtypeStruct((width, ff), BF16),
            jax.ShapeDtypeStruct((NZ, NX * NY, per, width), BF16),
        ],
        scratch_shapes=[pltpu.VMEM((count, width), F32), pltpu.VMEM((count, width), F32)],
        compiler_params=pltpu.CompilerParams(vmem_limit_bytes=48 * 1024 * 1024),
        cost_estimate=BRIEF,
        name="ffn_both",
    )(rows, dy, miss, router_t, w_in, w_out)


def norm_back_block(vector, gain, upstream):
    inverse = lax.rsqrt(jnp.mean(vector * vector, -1, keepdims=True) + EPS)
    scaled = upstream * gain
    grad_gain = jnp.sum(upstream * vector * inverse, 0, keepdims=True)
    grad_in = inverse * scaled - vector * (inverse * inverse * inverse) * jnp.mean(
        scaled * vector, -1, keepdims=True
    )
    return grad_in, grad_gain


def add_up(ref, value):
    @pl.when(pl.program_id(0) == 0)
    def _():
        ref[...] = value

    @pl.when(pl.program_id(0) > 0)
    def _():
        ref[...] += value


def middle_bwd_kernel(
    place_ref, m0_ref, m1_ref, m2_ref, m3_ref, middle_ref, up_ref, gain_ref, proj_ref,
    grad_ref, branch_ref, mixed_ref, gain_grad_ref,
):
    count = place_ref.shape[0]
    rows = jnp.concatenate([m0_ref[...], m1_ref[...], m2_ref[...], m3_ref[...]], 0)
    hot = place_ref[...] == lax.broadcasted_iota(jnp.int32, (count, rows.shape[0]), 1)
    normed_grad = dot(hot.astype(F32).astype(BF16), rows)
    grad, gain_grad = norm_back_block(middle_ref[...], gain_ref[...], normed_grad)
    grad = up_ref[...].astype(F32) + grad
    grad_ref[...] = grad
    branch = grad.astype(BF16)
    branch_ref[...] = branch
    mixed_ref[...] = dot(branch, proj_ref[...], ((1,), (1,))).astype(BF16)
    add_up(gain_grad_ref, gain_grad)


def middle_bwd(place, parts, middle, up, gain, proj):
    tok, width = middle.shape
    half = proj.shape[0]
    cap = BLK // 2
    whole = lambda i: (0, 0)
    block = lambda i: (i, 0)
    return pl.pallas_call(
        middle_bwd_kernel,
        grid=(tok // BLK,),
        in_specs=[pl.BlockSpec((BLK, 1), block)]
        + [pl.BlockSpec((cap, width), block)] * 4
        + [
            pl.BlockSpec((BLK, width), block),
            pl.BlockSpec((BLK, width), block),
            pl.BlockSpec((1, width), whole),
            pl.BlockSpec((half, width), whole),
        ],
        out_specs=[
            pl.BlockSpec((BLK, width), block),
            pl.BlockSpec((BLK, width), block),
            pl.BlockSpec((BLK, half), block),
            pl.BlockSpec((1, width), whole),
        ],
        out_shape=[
            jax.ShapeDtypeStruct((tok, width), F32),
            jax.ShapeDtypeStruct((tok, width), BF16),
            jax.ShapeDtypeStruct((tok, half), BF16),
            jax.ShapeDtypeStruct((1, width), F32),
        ],
        compiler_params=pltpu.CompilerParams(vmem_limit_bytes=32 * 1024 * 1024),
        cost_estimate=BRIEF,
        name="middle_bwd",
    )(place, *parts, middle, up, gain[None], proj)


def first_bwd_kernel(
    place_ref, own_ref, near_ref, stream_ref, grad_ref, gain_ref, gate_ref,
    up_ref, made_ref, gain_grad_ref,
):
    count = place_ref.shape[0]
    first_grad = own_ref[...].astype(F32) + near_ref[...].astype(F32)
    grad, gain_grad = norm_back_block(stream_ref[...], gain_ref[...], first_grad)
    grad = grad_ref[...] + grad
    up_ref[...] = grad
    hot = place_ref[...] == lax.broadcasted_iota(jnp.int32, (count, BLK), 1)
    gated = (gate_ref[...] * grad).astype(BF16)
    made = dot(hot.astype(F32).astype(BF16), gated, ((0,), (0,)))
    made_ref[...] = made[: made_ref.shape[0]].astype(BF16)
    add_up(gain_grad_ref, gain_grad)


def first_bwd(place, own, near, stream, grad, gain, gate):
    tok, width = stream.shape
    cap = BLK // 2
    whole = lambda i: (0, 0)
    block = lambda i: (i, 0)
    wide = pl.BlockSpec((BLK, width), block)
    return pl.pallas_call(
        first_bwd_kernel,
        grid=(tok // BLK,),
        in_specs=[
            pl.BlockSpec((BLK, 1), block), wide, wide, wide, wide,
            pl.BlockSpec((1, width), whole), pl.BlockSpec((BLK, 1), block),
        ],
        out_specs=[wide, pl.BlockSpec((cap, width), block), pl.BlockSpec((1, width), whole)],
        out_shape=[
            jax.ShapeDtypeStruct((tok, width), F32),
            jax.ShapeDtypeStruct((tok // 2, width), BF16),
            jax.ShapeDtypeStruct((1, width), F32),
        ],
        compiler_params=pltpu.CompilerParams(vmem_limit_bytes=32 * 1024 * 1024),
        cost_estimate=BRIEF,
        name="first_bwd",
    )(place, own, near, stream, grad, gain[None], gate)


def pack_kernel(normed_ref, qkv_ref, mixed_ref, branch_ref, small_ref, out_ref):
    wide = qkv_ref.shape[1]
    rows = mixed_ref.shape[1]
    half = branch_ref.shape[1] // 2
    out_ref[:, :wide] = dot(normed_ref[...], qkv_ref[...], ((0,), (0,))).astype(BF16)
    proj = dot(mixed_ref[...], branch_ref[...], ((0,), (0,))).astype(BF16)
    out_ref[:rows, wide : wide + half] = proj[:, :half]
    out_ref[rows:, wide : wide + half] = proj[:, half:]
    out_ref[:, wide + half :] = small_ref[...]


def pack_table(normed, qkv_grad, mixed, branch_grad, small):
    columns = qkv_grad.shape[1] + branch_grad.shape[1] // 2 + small.shape[1]
    return pl.pallas_call(
        pack_kernel,
        out_shape=jax.ShapeDtypeStruct((normed.shape[1], columns), BF16),
        compiler_params=pltpu.CompilerParams(vmem_limit_bytes=40 * 1024 * 1024),
        cost_estimate=BRIEF,
        name="pack_table",
    )(normed, qkv_grad, mixed, branch_grad, small)


def rep_index(x, yh, z):
    return ((x % NX) * NY + yh % NY) * NZ + z % NZ


def rep_shift(dx, dy, dz):
    return [
        (rep_index(x, y, z), rep_index(x + dx, y + dy, z + dz))
        for x in range(NX)
        for y in range(NY)
        for z in range(NZ)
    ]


def y_shift(dy, flip):
    reps = NX * NY * NZ
    pairs = []
    for x in range(NX):
        for yh in range(NY):
            for z in range(NZ):
                for yl in range(2):
                    for core in range(2):
                        y = (yh * 2 + yl + dy) % 4
                        source = (yl * 2 + core) * reps + rep_index(x, yh, z)
                        target = ((y % 2) * 2 + (core ^ flip)) * reps + rep_index(x, y // 2, z)
                        pairs.append((source, target))
    return pairs


def swap(value, bits):
    return lax.ppermute(value, "shard", [(s, s ^ bits) for s in range(4)])


def along_y(value, dy, flip):
    return lax.ppermute(value, ("shard", "rep"), y_shift(dy, flip))


def spread(value):
    near = swap(value, 1)
    far = swap(value, 2)
    return (value, near, far, swap(far, 1))


def in_order(values, me):
    rows = values[0].shape[0]
    whole = jnp.zeros((4 * rows,) + values[0].shape[1:], values[0].dtype)
    for r, value in enumerate(values):
        whole = lax.dynamic_update_slice_in_dim(whole, value, (me ^ r) * rows, 0)
    return whole


def take(array, index, axis=0):
    return lax.dynamic_index_in_dim(array, index, axis, keepdims=False)


def after(values, on):
    return lax.optimization_barrier((values, on))[0]


def exchange(array, axis, here, size, shift):
    got = [take(array, here, axis)]
    for step in range(1, size):
        got.append(lax.ppermute(take(array, (here + step) % size, axis), "rep", shift(step)))
    return got


def total(parts):
    return sum(part.astype(F32) for part in parts)


def x_parts(array, axis, place):
    return exchange(array, axis, place[0], NX, lambda s: rep_shift(s, 0, 0))


def y_parts(array, axis, place):
    return exchange(array, axis, place[1], NY, lambda s: rep_shift(0, s, 0))


def z_parts(array, axis, place):
    return exchange(array, axis, place[2], NZ, lambda s: rep_shift(0, 0, s))


def x_groups():
    return [[rep_index(x, y, z) for x in range(NX)] for y in range(NY) for z in range(NZ)]


def z_groups():
    return [[rep_index(x, y, z) for z in range(NZ)] for x in range(NX) for y in range(NY)]


def inner_first(inner):
    return lax.psum_scatter(
        inner, "rep", scatter_dimension=0, tiled=True, axis_index_groups=x_groups()
    )


def inner_y(part, place):
    return y_parts(part.reshape(NY, part.shape[0] // NY, part.shape[1]), 0, place)


def outer_first(outer):
    return lax.all_to_all(
        outer, "rep", split_axis=0, concat_axis=0, tiled=True, axis_index_groups=z_groups()
    )


def outer_sum(parts):
    return jnp.sum(parts.astype(F32), 0).astype(BF16)


def outer_y(parts, place):
    part = outer_sum(parts)
    return y_parts(part.reshape((NX, NY) + part.shape[1:]), 1, place)


def on_device(
    tokens,
    lengths,
    routes,
    attn_in,
    attn_proj,
    norm_first,
    norm_second,
    rel_bias,
    router,
    expert_in,
    expert_out,
    cotangent,
):
    me = lax.axis_index("shard")
    rep = lax.axis_index("rep")
    place = (rep // (NY * NZ), (rep // NZ) % NY, rep % NZ)
    core = me & 1
    odd = core == 1
    levels, own_rows, width3 = attn_in.shape
    width = width3 // 3
    half = width // 2
    tok = 4 * BLK
    heads = rel_bias.shape[2]
    heads_own = heads // 2
    buckets = rel_bias.shape[1]
    experts = router.shape[2]
    cap = BLK // 2

    def column_halves(block):
        parts = [block[..., i * half : (i + 1) * half] for i in range(6)]
        low = jnp.concatenate(parts[0::2], -1)
        high = jnp.concatenate(parts[1::2], -1)
        return jnp.where(odd, high, low), jnp.where(odd, low, high)

    cut = own_rows // 2
    route_row = jnp.zeros((16, width), BF16).at[0, :BLK].set(routes[0].astype(BF16))

    def fetch(own, axis):
        low = lax.slice_in_dim(own, 0, cut, axis=axis)
        high = lax.slice_in_dim(own, cut, 2 * cut, axis=axis)
        return along_y(low, 1, 0), along_y(high, -1, 0)

    def build_qkv(own, far):
        mine, others = column_halves(own)
        far_mine, far_others = column_halves(jnp.concatenate(far, 0))
        return in_order((mine, swap(others, 1), far_mine, swap(far_others, 1)), me)

    def build_proj(own, far):
        far = jnp.concatenate(far, 1)
        near = swap(jnp.stack([own, far], 0), 1)
        return [
            in_order((own[level], near[0, level], far[level], near[1, level]), me)
            for level in range(levels)
        ]

    w_qkv0 = build_qkv(attn_in[0], fetch(attn_in[0], 0))
    token_parts = spread(jnp.concatenate([tokens[0], route_row], 0))
    x0 = in_order([part[:BLK] for part in token_parts], me)
    route_parts = [part[BLK, :BLK].astype(jnp.int32) for part in token_parts]
    far_proj = fetch(after(attn_proj, w_qkv0), 1)

    position = jnp.arange(tok, dtype=jnp.int32)
    ends = jnp.cumsum(lengths[0])
    doc = jnp.sum((position[:, None] >= ends[None, :]).astype(jnp.int32), -1).astype(F32)
    docq, dock = doc[:, None], doc[None, :]
    own_bias = jnp.where(odd, rel_bias[:, :, heads_own:], rel_bias[:, :, :heads_own])
    turn = jnp.arange(2 * BLK, dtype=jnp.int32)
    line_offset = (
        BLK * (jnp.arange(8, dtype=jnp.int32) - 2)[:, None]
        + jnp.where(turn < BLK, turn, turn - 2 * BLK)[None]
    )
    line_hot = (
        bucket_of(line_offset)[None] == jnp.arange(buckets, dtype=jnp.int32)[:, None, None]
    ).astype(F32)
    lines = jnp.einsum("lbh,bdm->lhdm", own_bias, line_hot, precision=HIGH)
    lines = lines.reshape(levels, heads_own // 2, 2, 8, 2 * BLK)
    route = in_order([part[None] for part in route_parts], me)
    onehot = (route[..., None] == jnp.arange(experts, dtype=jnp.int32)).astype(jnp.int32)
    slot = jnp.sum(jnp.cumsum(onehot, axis=1) * onehot, -1) - 1
    dispatch = (
        (route == me)[:, None, :] & (slot[:, None, :] == jnp.arange(cap)[None, :, None])
    ).astype(BF16)
    at_slot = jnp.arange(4, dtype=jnp.int32)[:, None] * cap + slot
    collect = [
        (
            (route.reshape(tok) == (me ^ r))[:, None]
            & (at_slot.reshape(tok)[:, None] == jnp.arange(4 * cap)[None, :])
        ).astype(BF16)
        for r in range(4)
    ]
    chosen = onehot.reshape(tok, experts).astype(F32)
    spot = ((route ^ me) * cap + slot).reshape(tok, 1)

    router_ts = [
        jnp.pad(router[level].T, ((0, BLK - experts), (0, 0))) for level in range(levels)
    ]
    router_ts, spot, collect, chosen, x0 = lax.optimization_barrier(
        (router_ts, spot, collect, chosen, x0)
    )

    def rows_of(stream):
        return jnp.einsum(
            "bct,btd->bcd", dispatch, stream.reshape(4, BLK, -1), preferred_element_type=F32
        ).reshape(4 * cap, -1)

    def gathered(parts):
        return (
            dot(collect[0], parts[0])
            + dot(collect[1], parts[1])
            + dot(collect[2], parts[2])
            + dot(collect[3], parts[3])
        )

    def cols_of(array):
        return lax.dynamic_slice_in_dim(array, me * own_rows, own_rows, 1)

    saved = []
    misses = []
    w_qkv = [w_qkv0]
    stream = x0.astype(F32)
    for level in range(levels):
        normed = rms_norm(stream, norm_first[level]).astype(BF16)
        qkv = dot(normed, w_qkv[level]).astype(BF16)
        if level > 0:
            qkv, cot_own = lax.optimization_barrier((qkv, cotangent[0]))
            cot = in_order(spread(cot_own), me)
        o_own, probs = attn_fwd(qkv, lines[level], docq, dock)
        if level == 0:
            w_proj = build_proj(*after((attn_proj, far_proj), o_own))
            next_in = after(attn_in[1], o_own)
            next_far = fetch(next_in, 0)
        o_near = swap(o_own, 1)
        mixed = jnp.concatenate(
            [jnp.where(odd, o_near, o_own), jnp.where(odd, o_own, o_near)], 1
        )
        middle = stream + dot(mixed, w_proj[level])
        normed_two = rms_norm(middle, norm_second[level]).astype(BF16)
        logits = dot(normed_two, router[level])
        route_probs = jax.nn.softmax(logits, -1)
        gate = jnp.sum(route_probs * chosen, -1)
        rows = rows_of(normed_two).astype(BF16)
        slot_probs = jnp.einsum(
            "bct,bte->bce", dispatch, route_probs.reshape(4, BLK, experts).astype(BF16),
            preferred_element_type=F32,
        ).reshape(4 * cap, experts)
        miss = jnp.pad(
            (jnp.arange(experts) == me).astype(F32)[None] - slot_probs,
            ((0, 0), (0, BLK - experts)),
        )
        misses.append(miss)
        saved.append(
            (stream, normed, qkv, o_own, probs, mixed, middle, normed_two, route_probs, gate, rows)
        )
        if level < levels - 1:
            made = ffn_fwd(rows, expert_in, expert_out, level)
            w_qkv.append(build_qkv(*after((next_in, next_far), made)))
            made_parts = spread(made)
            w_proj_owns = [lax.dynamic_slice_in_dim(w, core * half, half, 0) for w in w_proj]
            middle, gate, misses, w_proj_owns, far_made = lax.optimization_barrier(
                (middle, gate, misses, w_proj_owns, made_parts[2])
            )
            made_parts = made_parts[:2] + (far_made,) + made_parts[3:]
            stream = middle + gate[:, None] * gathered(made_parts)

    def go_home(made, middle, gate):
        blocks = made.reshape(4, cap, width)
        home = [take(blocks, me)] + [swap(take(blocks, me ^ r), r) for r in (1, 2, 3)]
        own_route, own_slot = take(route, me), take(slot, me)
        back = sum(
            dot(
                (
                    (own_route == (me ^ r))[:, None]
                    & (own_slot[:, None] == jnp.arange(cap)[None, :])
                ).astype(BF16),
                home[r],
            )
            for r in range(4)
        )
        own_gate = lax.dynamic_slice_in_dim(gate, me * BLK, BLK, 0)
        own_after = lax.dynamic_slice_in_dim(middle, me * BLK, BLK, 0)
        result = (own_after + own_gate[:, None] * back).astype(BF16)[None]
        return result

    def pack(normed, mixed, normed_two, branch_grad, qkv_grad, bias_sums, message_parts,
             route_probs, grad_first, grad_second):
        chip_rows = lambda array, axis: lax.dynamic_slice_in_dim(
            array, (me >> 1) * 2 * own_rows, 2 * own_rows, axis
        )
        token_gate_grad = sum(
            dot(collect[r], message_parts[r][4 * cap :, : 4 * cap], ((1,), (1,))) for r in range(4)
        )[:, :1]
        logit_grad = token_gate_grad * (chosen - route_probs)
        own_vec = lambda vec: lax.dynamic_slice_in_dim(vec, me * own_rows, own_rows, 0)[:, None]
        grad_router = dot(cols_of(normed_two), logit_grad.astype(BF16), ((0,), (0,)))
        own = jnp.concatenate([own_vec(grad_first), own_vec(grad_second), grad_router], 1)
        own = jnp.where(
            (jnp.arange(2) == core)[:, None, None], own[None], jnp.zeros_like(own)[None]
        )
        count = after(jnp.arange(BLK, dtype=jnp.int32), branch_grad)
        offset = (
            BLK * (jnp.arange(5, dtype=jnp.int32) - 2)[:, None, None]
            + count[None, None, :]
            - count[None, :, None]
        )
        bucket_id = bucket_of(offset)
        bucket_hot = bucket_id[None] == jnp.arange(buckets, dtype=jnp.int32)[:, None, None, None]
        bias_own = jnp.einsum(
            "hdij,bdij->bh", bias_sums, bucket_hot.astype(BF16), preferred_element_type=F32
        )
        none = jnp.zeros_like(bias_own)
        bias_all = jnp.where(
            odd,
            jnp.concatenate([none, bias_own], 1),
            jnp.concatenate([bias_own, none], 1),
        ).reshape(-1)
        bias_rows = lax.dynamic_slice_in_dim(
            bias_all, (me >> 1) * bias_all.shape[0] // 2, bias_all.shape[0] // 2, 0
        ).reshape(2, 32, -1)
        per = own_rows // 32
        bias_rows = jnp.pad(bias_rows, ((0, 0), (0, 0), (0, per - bias_rows.shape[2])))
        small = jnp.concatenate([own, bias_rows.reshape(2, own_rows, 1)], 2)
        small = jnp.pad(small, ((0, 0), (0, 0), (0, BLK - small.shape[2]))).astype(BF16)
        table = pack_table(
            chip_rows(normed, 1), qkv_grad, cols_of(mixed), branch_grad, small.reshape(2 * own_rows, -1)
        )
        table = table.reshape(2, NX, NY, NZ * per, table.shape[1])
        return table

    upstream = cot
    packs = [None] * levels
    inner_parts = [None] * levels
    outer_parts = [None] * levels
    for level in reversed(range(levels)):
        (stream, normed, qkv, o_own, probs, mixed, middle, normed_two, route_probs, gate,
         rows) = saved[level]
        if level == levels - 1:
            made_grad = rows_of((gate[:, None] * upstream.astype(F32)).astype(BF16)).astype(BF16)
        w_proj_own = w_proj_owns[level]
        made_grad, upstream, w_proj_own, spot = lax.optimization_barrier(
            (made_grad, upstream, w_proj_own, spot)
        )
        made, message, inner, outer = ffn_both(
            rows, made_grad, misses[level], router_ts[level], expert_in, expert_out, level
        )
        message_parts = spread(message)
        far_part = message_parts[2]
        if level == levels - 1:
            last = (made, middle, gate)
        waited = (far_part,)
        if level < levels - 1:
            over = level + 1
            waited = (far_part, outer_parts[over], inner_parts[over])
        inner, outer, upstream, middle, route_probs, waited = lax.optimization_barrier(
            (inner, outer, upstream, middle, route_probs, waited)
        )
        inner_parts[level] = inner_first(inner)
        outer_parts[level] = outer_first(outer)
        if level < levels - 1:
            outer_parts[over] = outer_y(waited[1], place)
            inner_parts[over] = inner_y(waited[2], place)

        after_grad, branch_grad, mixed_grad, grad_second = middle_bwd(
            spot, message_parts, middle, upstream, norm_second[level], w_proj_own
        )
        grad_second = grad_second[0]
        qkv_grad, bias_sums = attn_bwd(qkv, probs, mixed_grad, o_own)
        if level < levels - 1:
            pending, stream = after((pending, stream), qkv_grad)
            packs[level + 1] = pack(*pending)
        first_part = dot(qkv_grad, w_qkv[level], ((1,), (1,))).astype(BF16)
        near_first = swap(first_part, 1)
        if level > 0:
            upstream, made_grad, grad_first = first_bwd(
                spot, first_part, near_first, stream, after_grad, norm_first[level],
                saved[level - 1][9][:, None],
            )
            grad_first = grad_first[0]
        else:
            input_side, grad_first = norm_back(
                stream, norm_first[level], first_part.astype(F32) + near_first.astype(F32)
            )
            upstream = after_grad + input_side
        pending = (normed, mixed, normed_two, branch_grad, qkv_grad, bias_sums, message_parts,
                   route_probs, grad_first, grad_second)
        if level < levels - 1:
            packs[level] = pack(*pending)

    own_parts = list(packs)

    outer_low, inner_low = after((outer_parts[0], inner_parts[0]), own_parts)
    outer_low = outer_sum(outer_low)
    inner_top, outer_top = after((inner_parts[1], outer_parts[1]), own_parts)
    last, packs = after((last, packs), outer_low)
    inner_top = total(inner_top).astype(BF16)
    outer_top = total(outer_top).astype(BF16)
    rows_in = inner_low.shape[0] // (NY * NZ)
    inner_all = jnp.concatenate(
        [
            inner_low.reshape(NY, NZ, rows_in, -1),
            inner_top.reshape(1, NZ, rows_in, -1),
        ],
        0,
    )
    outer_all = jnp.concatenate(
        [outer_low.reshape((NX, NY) + outer_low.shape[1:]), outer_top[:, None]], 1
    )
    inner_all = z_parts(inner_all, 1, place)
    outer_all = x_parts(outer_all, 0, place)
    packs = [y_parts(table, 2, place) for table in packs]
    inner_all, outer_all, packs, last = lax.optimization_barrier(
        (inner_all, outer_all, packs, last)
    )
    result = go_home(*last)
    inner_all = total(inner_all)
    outer_all = total(outer_all)
    inner_low = total(y_parts(inner_all[:NY].astype(BF16), 0, place))
    outer_low = total(y_parts(outer_all[:NY].astype(BF16), 0, place))
    expert_in_grad = jnp.stack([inner_low, inner_all[NY]], 0)[:, None]
    expert_out_grad = jnp.stack([outer_low, outer_all[NY]], 0)[:, None]
    table = jnp.stack([total(part).astype(BF16) for part in packs], 0)
    table = total(x_parts(table, 2, place)).astype(BF16)
    per = own_rows // 32
    table = total(z_parts(table.reshape(levels, 2, NZ, per, -1), 2, place))
    mine = take(table, core, 1)
    near = swap(take(table, core ^ 1, 1), 1)
    pieces = []
    for part in range(3):
        a = mine[..., part * half : (part + 1) * half]
        b = near[..., part * half : (part + 1) * half]
        pieces += [jnp.where(odd, b, a), jnp.where(odd, a, b)]
    attn_in_grad = jnp.concatenate(pieces, -1)
    at = width3 // 2
    attn_proj_grad = jnp.concatenate(
        [table[:, 0, :, at : at + half], table[:, 1, :, at : at + half]], -1
    )
    at += half
    few = buckets * heads // 128
    stacked = (
        attn_in_grad,
        attn_proj_grad,
        mine[:, :, at],
        mine[:, :, at + 1],
        mine[:, :few, at + 2 + experts] + near[:, :few, at + 2 + experts],
        mine[:, :, at + 2 : at + 2 + experts],
    )

    own_up = lax.dynamic_slice_in_dim(upstream, me * BLK, BLK, 0)
    tokens_grad = own_up.astype(BF16)[None]
    return (result, tokens_grad, *stacked, expert_in_grad, expert_out_grad)


def solution(mesh):
    return jax.shard_map(
        on_device,
        mesh=mesh,
        in_specs=(
            P("rep", "shard", None),
            P("rep", None),
            P("rep", "shard"),
            P(None, "shard", None),
            P(None, "shard", None),
            P(),
            P(),
            P(),
            P(),
            P(None, "shard", None, None),
            P(None, "shard", None, None),
            P("rep", "shard", None),
        ),
        out_specs=(
            P("rep", "shard", None),
            P("rep", "shard", None),
            P(None, ("shard", "rep"), None),
            P(None, ("shard", "rep"), None),
            P(None, ("shard", "rep")),
            P(None, ("shard", "rep")),
            P(None, ("shard", "rep")),
            P(None, ("shard", "rep"), None),
            P(None, "shard", "rep", None),
            P(None, "shard", "rep", None),
        ),
        check_vma=False,
    )
```
